32 devices in a mesh: groups: 2 (over y), blk: 4 (over z), head: 2 (over x), rep: 2 (over core).
Axes of the slice: x: 2, y: 2, z: 4, core: 2. Of those that a mesh axis runs over, the one named last changes fastest.
Arguments:
- merger_rows: bfloat16 [1536, 5120], P(('groups', 'blk')), parts along dimension 0, may hold values from -6 to 6
- out_weight: bfloat16 [5120, 8192], P('blk', ('head', 'rep')), may hold values from -0.078125 to 0.078125
- kv_weight: bfloat16 [8192, 2048], P(('head', 'rep')), may hold values from -0.09375 to 0.09375
- kv_bias: float32 [8, 256], P('head'), may hold values from -3 to 3
- merge_map: int32 [16, 96], P(('groups', 'blk', 'rep')), parts along dimension 0, may hold values from 0 to 95, each once within a row
- owner_map: int32 [192, 1], P(('groups', 'blk', 'rep')), parts along dimension 0, may hold values from 0 to 3; in each aligned block of 12 rows (0 to 11, 12 to 23, ...) at most 6 rows name the same one
- old_memory: bfloat16 [2048, 8, 8, 256], P(('groups', 'blk', 'rep'), None, 'head'), parts along dimension 0, may hold values from -4 to 4
- queries: bfloat16 [8, 8, 8, 1024], P(('groups', 'blk'), None, 'head'), parts along dimension 0, may hold values from -6 to 6
- retrieved: int32 [8, 32], P('groups'), parts along dimension 0, may hold values from 0 to 1119, as said below
Outputs:
- answer: bfloat16 [8, 8, 8, 1024], P(('groups', 'blk'), 'rep', 'head'), parts along dimension 0
- new_memory: bfloat16 [384, 8, 8, 256], P(('groups', 'blk', 'rep'), None, 'head'), parts along dimension 0
The draws below stay inside these ranges and needn't reach their ends.
There are 2 independent parts, one for each index of `groups`. The reference program is written for one: setup_inputs(seed, part) draws one part's arguments, and reference() takes and returns one part's arrays. A program takes and returns all parts, laid end to end along the dimension named above; an argument that names none is the same for every part. Nothing has to cross between parts.
Inputs may be any that keep to these rules, and one draw needn't show every extreme that they name: `merge_map`: each row of a group g is a permutation of 0 to 95. `owner_map`: in each aligned block of 12 rows (the new units of one index of blk and rep) no value appears more than 6 times. `retrieved`: each row holds 32 distinct ids: 24 stored units below 1024, then 8 new units from 1024 on.
All inputs are finite; a program needn't handle non-finite values.
Results may differ from the reference program's by a relative error of at most 0.025.
Values may be sent and summed in bfloat16 or wider, within the bound.
A program may use at most 192 MiB of HBM per device.

```python
import math
import jax
import jax.numpy as jnp
import numpy as np
from jax import lax

DV = 5120
DL = 8192
KVH = 8
QPK = 8
HD = 128
UNIT_TOK = 8
QTOK = 8
OLD_PICK = 24
NEW_PICK = 8
HALF = 96
NEWU = 12
CAP = 6
TOKENS = 768
OLD_UNITS = 1024
NEW_UNITS = 96
NQ = 4
TOPU = 32
N_BLK = 4
N_REP = 2


def designated_units(key):
    key = jax.random.fold_in(key, 11)
    order = jax.random.permutation(key, OLD_UNITS)
    return ((order - order[0]) % OLD_UNITS)[:NQ].astype(jnp.int32)


def draw_old_memory(key, part):
    key = jax.random.fold_in(key, 1)
    shape = (OLD_UNITS, UNIT_TOK, KVH, 2 * HD)
    memory = jax.random.truncated_normal(key, -4.0, 4.0, shape, jnp.float32)
    return memory.astype(jnp.bfloat16)


def draw_queries(key, part):
    key = jax.random.fold_in(key, 2)
    shape = (NQ, QTOK, KVH, QPK * HD)
    values = jax.random.truncated_normal(key, -4.0, 4.0, shape, jnp.float32)
    return values.astype(jnp.bfloat16)


def draw_retrieved(key, part):
    marks = designated_units(key)
    key = jax.random.fold_in(key, 3)
    old_keys = jax.random.split(jax.random.fold_in(key, 1), NQ)
    new_keys = jax.random.split(jax.random.fold_in(key, 2), NQ)

    def old_offsets(one_key):
        return jax.random.permutation(one_key, OLD_UNITS - 1)[:OLD_PICK - 1].astype(jnp.int32) + 1

    def new_picks(one_key):
        return jax.random.permutation(one_key, NEW_UNITS)[:NEW_PICK].astype(jnp.int32)
    offsets = jax.vmap(old_offsets)(old_keys)
    offsets = jnp.concatenate([jnp.zeros((NQ, 1), jnp.int32), offsets], axis=1)
    old_part = (marks[:, None] + offsets) % OLD_UNITS
    new_part = jax.vmap(new_picks)(new_keys)
    first_row = (new_part[0] + (NEW_UNITS - 1 - new_part[0, 0])) % NEW_UNITS
    new_part = new_part.at[0].set(first_row)
    return jnp.concatenate([old_part, new_part + OLD_UNITS], axis=1).astype(jnp.int32)


def with_spikes(result, key, source, target, parts, factor):
    def block_of(position):
        return (jnp.arange(result.shape[position]) // (result.shape[position] // parts)).reshape((-1,) + (1,) * (result.ndim - 1 - position))

    first = jax.random.permutation(key, parts)[block_of(target)]
    far = (block_of(target) + parts // 2) % parts
    return jnp.where((block_of(source) == first) | (block_of(source) == far), factor * result, result)


def block_levels(own_key, dims, cuts, least, top_value):
    loudness, own = 1.0, jax.random.fold_in(own_key, 6)
    for dim, parts in cuts:
        heights = jnp.exp(jax.random.uniform(jax.random.fold_in(own, dim), (parts,), jnp.float32, least / len(cuts), top_value / len(cuts)))
        loudness = loudness * jnp.repeat(heights, dims[dim] // parts).reshape([-1 if axis == dim else 1 for axis in range(len(dims))])
    return loudness


def routed_block(stream_key, own, number, rows, count, top, reach, lean):
    order = jax.random.permutation(stream_key, count)
    heavy_load, common = load_shares(count, rows * top, reach, lean, True), load_shares(count, rows * top, reach, lean, False)
    places = jnp.arange(count)

    def named(sizes, offset_by):
        used = int((sizes > 0).sum())
        fixed = max(1, used // 4)
        moved = fixed + (places - fixed + offset_by * (used - fixed)) % max(1, count - fixed)
        return jnp.zeros((count,), jnp.int32).at[order[jnp.where(places < fixed, places, moved)]].set(jnp.asarray(sizes, jnp.int32))

    sizes = jnp.where(number % 4 == 0, named(heavy_load, number // 4), named(common, number - number // 4 - 1))
    mixed = jax.random.permutation(jax.random.fold_in(own, 3), count)
    donor, sink = mixed[0:count // 2 * 2:2], mixed[1:count // 2 * 2:2]
    room = jnp.minimum(sizes[donor] - 1, reach - sizes[sink]) // 2
    room = jnp.where((donor == order[0]) | (sink == order[0]) | (sizes[sink] == 0), 0, jnp.maximum(room, 0))
    moved = jax.random.randint(jax.random.fold_in(own, 4), (count // 2,), 0, 1 << 20) % (room + 1)
    sizes = sizes.at[donor].add(-moved).at[sink].add(moved)
    members = jnp.searchsorted(jnp.cumsum(sizes), jnp.arange(rows * top), side="right").astype(jnp.int32)
    listing = members.reshape(top, rows).T
    listing = listing[jax.random.permutation(jax.random.fold_in(own, 1), rows)]
    offset_by = jax.random.randint(jax.random.fold_in(own, 2), (rows, 1), 0, top)
    return jnp.take_along_axis(listing, (jnp.arange(top)[None, :] + offset_by) % top, axis=1)


def load_shares(count, total, bound, skew, full):
    weights = [(1 << 20) // math.isqrt(standing ** skew) + 1 for standing in range(1, count + 1)]
    largest = bound if full else min(bound, max(-(-total // count), total * weights[0] // sum(weights)))
    least = 1 if total - largest >= count - 1 else 0
    holding, surplus = [largest] + [least] * (count - 1), total - largest - least * (count - 1)
    while surplus > 0:
        free = [i for i in range(1, count) if holding[i] < largest] or [i for i in range(1, count) if holding[i] < bound]
        pool, remaining = sum([weights[i] for i in free]), surplus
        for i in free:
            addition = min(bound - holding[i], max(1, remaining * weights[i] // pool), surplus)
            holding[i] = holding[i] + addition
            surplus = surplus - addition
    return np.array(holding)


def scatter_about(stream_key, shape, spread, limit, pieces=(), kind=jnp.bfloat16):
    array = jax.random.normal(stream_key, shape, jnp.float32) * spread
    if len(pieces) > 0:
        array = block_levels(stream_key, shape, pieces, -0.22, 0.18) * array
    return jnp.clip(array, min=-limit, max=limit).astype(kind)


def gaussian_with(key, dims, spread, reach, cuts, heavy, kind=jnp.bfloat16):
    values = spread * jax.random.normal(key, dims, jnp.float32)
    if cuts:
        values = values * block_levels(key, dims, cuts, -0.22, 0.18)
    return jnp.clip(with_spikes(values, jax.random.fold_in(key, 3), *heavy), -reach, reach).astype(kind)


def setup_inputs(seed: int = 0, part: int = 0) -> dict:
    streams_of = jax.random.split(jax.random.key(seed), 10)
    own_keys = jax.random.split(jax.random.fold_in(streams_of[9], part), 10)
    merger_rows = scatter_about(own_keys[0], (TOKENS, DV), 1.0, 6.0, ((0, 4),))
    out_weight = scatter_about(streams_of[1], (DV, DL), DV ** -0.5, 0.078125, ((0, 4), (1, 4)))
    kv_weight = gaussian_with(streams_of[2], (DL, KVH * 2 * HD), DL ** -0.5, 0.09375, ((0, 4),), (0, 1, 4, 2.0))
    kv_bias = scatter_about(streams_of[3], (KVH, 2 * HD), 0.5, 3.0, ((0, 2),), jnp.float32)
    merge_map = jax.vmap(lambda own: jax.random.permutation(own, HALF))(jax.random.split(own_keys[4], (N_BLK * N_REP))).reshape((N_BLK * N_REP, HALF)).astype(jnp.int32)
    owner_map_keys = jax.random.split(jax.random.fold_in(own_keys[5], 1), NEW_UNITS // NEWU)
    owner_map_turns = jax.random.permutation(jax.random.fold_in(own_keys[5], 3), NEW_UNITS // NEWU)
    owner_map = jax.vmap(lambda own, number: routed_block(jax.random.fold_in(own_keys[5], 2), own, number, NEWU, N_BLK, 1, CAP, 2))(owner_map_keys, owner_map_turns).reshape((NEW_UNITS, 1))
    old_memory = draw_old_memory(jax.random.fold_in(jax.random.fold_in(streams_of[9], part), 71), part)
    queries = draw_queries(jax.random.fold_in(jax.random.fold_in(streams_of[9], part), 71), part)
    retrieved = draw_retrieved(jax.random.fold_in(jax.random.fold_in(streams_of[9], part), 71), part)
    return {"merger_rows": merger_rows, "out_weight": out_weight, "kv_weight": kv_weight, "kv_bias": kv_bias, "merge_map": merge_map, "owner_map": owner_map, "old_memory": old_memory, "queries": queries, "retrieved": retrieved}


def reference(merger_rows, out_weight, kv_weight, kv_bias, merge_map, owner_map, old_memory, queries, retrieved):
    group_total = N_BLK * N_REP
    visual = jnp.dot(merger_rows, out_weight, preferred_element_type=jnp.float32).astype(jnp.bfloat16)
    keyval = jnp.dot(visual, kv_weight, preferred_element_type=jnp.float32).reshape(TOKENS, KVH, 2 * HD)
    keyval = (keyval + kv_bias[None]).astype(jnp.bfloat16)
    halves = keyval.reshape(group_total, HALF, KVH, 2 * HD)
    ordered = jnp.take_along_axis(halves, merge_map.astype(jnp.int32)[:, :, None, None], axis=1)
    new_units = ordered.reshape(NEW_UNITS, UNIT_TOK, KVH, 2 * HD)
    owners = owner_map[:, 0].astype(jnp.int32).reshape(group_total, NEWU)
    same_owner = owners[:, :, None] == owners[:, None, :]
    positions = jnp.arange(NEWU, dtype=jnp.int32)
    earlier = positions[None, :] < positions[:, None]
    ranks = jnp.sum((same_owner & earlier[None]).astype(jnp.int32), axis=2)
    sources = jnp.arange(group_total, dtype=jnp.int32)[:, None]
    slot_rows = ((owners * N_REP + sources % N_REP) * N_BLK + sources // N_REP) * CAP + ranks
    new_memory = jnp.zeros((group_total * N_BLK * CAP, UNIT_TOK, KVH, 2 * HD), jnp.bfloat16)
    new_memory = new_memory.at[slot_rows.reshape(-1).astype(jnp.int32)].set(new_units)
    every_unit = jnp.concatenate([old_memory, new_units], axis=0)

    def answer_one(index):
        chosen = jnp.take(every_unit, retrieved[index].astype(jnp.int32), axis=0)
        chosen = chosen.reshape(TOPU * UNIT_TOK, KVH, 2 * HD).astype(jnp.float32)
        query = queries[index].reshape(QTOK, KVH, QPK, HD).astype(jnp.float32)
        scores = jnp.einsum('qkhd,tkd->qkht', query, chosen[..., :HD]) * (HD ** -0.5)
        peak = jnp.max(scores, axis=-1, keepdims=True)
        weights = jnp.exp(scores - peak)
        total = jnp.sum(weights, axis=-1)
        rounded = lax.optimization_barrier(weights.astype(jnp.bfloat16)).astype(jnp.float32)
        output = jnp.einsum('qkht,tkd->qkhd', rounded, chosen[..., HD:]) / total[..., None]
        return output.reshape(QTOK, KVH, QPK * HD).astype(jnp.bfloat16)

    answer = lax.map(answer_one, jnp.arange(NQ, dtype=jnp.int32))
    return answer, new_memory
```

```python
import jax
import jax.numpy as jnp
from jax import lax
from jax.sharding import PartitionSpec as P

KVH = 8
UNIT_TOK = 8


def project(merger_rows, out_weight, kv_weight, blocks, head_groups, copies):
    rows = merger_rows.shape[0]
    depth = out_weight.shape[0]
    split = merger_rows.reshape(rows, blocks, depth).transpose(1, 0, 2)
    features = lax.all_to_all(split, "blk", split_axis=0, concat_axis=0, tiled=True)
    visual = jnp.dot(
        features.reshape(blocks * rows, depth), out_weight, preferred_element_type=jnp.float32
    ).astype(jnp.bfloat16)
    partial = jnp.dot(visual, kv_weight, preferred_element_type=jnp.float32).astype(jnp.bfloat16)
    cols = kv_weight.shape[1] // head_groups
    partial = partial.reshape(blocks, copies, rows // copies, head_groups, cols)
    partial = partial.transpose(0, 3, 1, 2, 4).reshape(-1, rows // copies, cols)
    return lax.psum_scatter(
        partial, ("blk", "head", "rep"), scatter_dimension=0, tiled=True
    ).reshape(rows // copies, cols)


def body(
    merger_rows,
    out_weight,
    kv_weight,
    kv_bias,
    merge_map,
    owner_map,
    old_memory,
    queries,
    retrieved,
):
    blocks = lax.axis_size("blk")
    copies = lax.axis_size("rep")
    head_groups = lax.axis_size("head")
    local_heads = KVH // head_groups
    width = kv_weight.shape[1] // KVH
    head_size = width // 2
    group_index = lax.axis_index("blk") * copies + lax.axis_index("rep")

    keyval = project(merger_rows, out_weight, kv_weight, blocks, head_groups, copies)
    half_rows = keyval.shape[0]
    keyval = (keyval.astype(jnp.float32) + kv_bias.reshape(1, -1)).astype(jnp.bfloat16)

    unit_count = half_rows // UNIT_TOK
    capacity = 2 * ((unit_count + blocks - 1) // blocks)
    owners = owner_map[:, 0]
    positions = jnp.arange(unit_count, dtype=jnp.int32)
    same_owner = owners[:, None] == owners[None, :]
    earlier = positions[None, :] < positions[:, None]
    ranks = jnp.sum((same_owner & earlier).astype(jnp.int32), axis=1)
    slots = owners * capacity + ranks
    row_slots = jnp.repeat(slots * UNIT_TOK, UNIT_TOK) + jnp.tile(
        jnp.arange(UNIT_TOK, dtype=jnp.int32), unit_count
    )
    placed_at = merge_map[0][:, None] == jnp.arange(half_rows, dtype=jnp.int32)[None, :]
    row_target = jnp.sum(jnp.where(placed_at, row_slots[:, None], 0), axis=0)
    slot_rows = blocks * capacity * UNIT_TOK
    select = row_target[None, :] == jnp.arange(slot_rows, dtype=jnp.int32)[:, None]
    send = jnp.dot(select.astype(jnp.bfloat16), keyval, preferred_element_type=jnp.float32)
    send = send.astype(jnp.bfloat16).reshape(blocks, capacity * UNIT_TOK, keyval.shape[1])
    arrived = lax.all_to_all(send, "blk", split_axis=0, concat_axis=0, tiled=True)
    new_memory = arrived.reshape(blocks * capacity, UNIT_TOK, local_heads, width)

    old_count = old_memory.shape[0]
    old_ids = group_index * old_count + jnp.arange(old_count, dtype=jnp.int32)
    new_ids = old_count * blocks * copies + group_index * unit_count + positions
    old_listed = jnp.any(retrieved[:, :, None] == old_ids[None, None, :], axis=1)
    new_listed = jnp.any(retrieved[:, :, None] == new_ids[None, None, :], axis=1)
    slot_listed = jnp.repeat(new_listed, UNIT_TOK, axis=1)
    row_listed = jnp.any(slot_listed[:, :, None] & placed_at[None], axis=1)
    mask = jnp.concatenate([jnp.repeat(old_listed, UNIT_TOK, axis=1), row_listed], axis=1)

    query_rows = queries.shape[1]
    per_head = queries.shape[3] // head_size
    slice_rows = query_rows // copies
    asked = lax.all_gather(queries, "blk", axis=0, tiled=True)
    questions = asked.shape[0]
    asked = asked.reshape(questions, query_rows, local_heads, per_head, head_size)
    old_flat = old_memory.reshape(-1, local_heads, width)
    flat = jnp.concatenate([old_flat, keyval.reshape(half_rows, local_heads, width)], axis=0)
    keys = flat[..., :head_size]
    values = flat[..., head_size:]
    wide_mask = mask[None, :, None, None, :]
    scores = jnp.einsum("aqkhd,tkd->kaqht", asked, keys, preferred_element_type=jnp.float32)
    scores = jnp.where(wide_mask, scores * head_size ** (-0.5), -1e30)
    peak = jnp.max(scores, axis=-1)
    weights = jnp.where(wide_mask, jnp.exp(scores - peak[..., None]), 0.0)
    total = jnp.sum(weights, axis=-1)
    output = jnp.einsum(
        "kaqht,tkd->kaqhd", weights.astype(jnp.bfloat16), values, preferred_element_type=jnp.float32
    )

    def by_holder(part):
        part = part.reshape((local_heads, questions, copies, slice_rows) + part.shape[3:])
        part = jnp.moveaxis(part, 0, 3)
        return part.reshape((questions * copies, slice_rows * local_heads * per_head) + part.shape[5:])

    answer_rows = slice_rows * local_heads * per_head
    stat_rows = -(-answer_rows // head_size)
    spare = ((0, 0), (0, stat_rows * head_size - answer_rows))
    stats = jnp.stack([jnp.pad(by_holder(peak), spare), jnp.pad(by_holder(total), spare)], axis=1)
    partial = jnp.concatenate(
        [by_holder(output), stats.reshape(questions * copies, 2 * stat_rows, head_size)], axis=1
    )
    partial = lax.all_to_all(partial, ("blk", "rep"), split_axis=0, concat_axis=0, tiled=True)
    outputs = partial[:, :answer_rows]
    stats = partial[:, answer_rows:].reshape(-1, 2, stat_rows * head_size)[..., :answer_rows]
    scale = jnp.exp(stats[:, 0] - jnp.max(stats[:, 0], axis=0, keepdims=True))
    total = jnp.sum(stats[:, 1] * scale, axis=0)
    result = jnp.sum(outputs * scale[..., None], axis=0) / total[:, None]
    answer = result.reshape(1, slice_rows, local_heads, per_head * head_size).astype(jnp.bfloat16)
    return (answer, new_memory)


def solution(mesh):
    placed = (
        P(("groups", "blk"), None),
        P("blk", ("head", "rep")),
        P(("head", "rep"), None),
        P("head", None),
        P(("groups", "blk", "rep"), None),
        P(("groups", "blk", "rep"), None),
        P(("groups", "blk", "rep"), None, "head", None),
        P(("groups", "blk"), None, "head", None),
        P("groups", None),
    )
    return jax.shard_map(
        body,
        mesh=mesh,
        in_specs=placed,
        out_specs=(
            P(("groups", "blk"), "rep", "head", None),
            P(("groups", "blk", "rep"), None, "head", None),
        ),
        check_vma=False,
    )
```

```python
import jax
import jax.numpy as jnp
from jax import lax
from jax.experimental import pallas as pl
from jax.experimental.pallas import tpu as pltpu
from jax.sharding import PartitionSpec as P

KVH = 8
UNIT_TOK = 8


def project(merger_rows, out_weight, kv_weight, blocks, head_groups, copies):
    rows = merger_rows.shape[0]
    depth = out_weight.shape[0]
    split = merger_rows.reshape(rows, blocks, depth).transpose(1, 0, 2)
    features = lax.all_to_all(split, "blk", split_axis=0, concat_axis=0, tiled=True)
    visual = jnp.dot(
        features.reshape(blocks * rows, depth), out_weight, preferred_element_type=jnp.float32
    ).astype(jnp.bfloat16)
    partial = jnp.dot(visual, kv_weight, preferred_element_type=jnp.float32).astype(jnp.bfloat16)
    cols = kv_weight.shape[1] // head_groups
    partial = partial.reshape(blocks, copies, rows // copies, head_groups, cols)
    partial = partial.transpose(0, 3, 1, 2, 4).reshape(-1, rows // copies, cols)
    return lax.psum_scatter(
        partial, ("blk", "head", "rep"), scatter_dimension=0, tiled=True
    ).reshape(rows // copies, cols)


TILE = 512
ORDER = (0, 2, 3, 1)
VMEM_BYTES = 48 * 1024 * 1024


def partner(block, k):
    if k == 0:
        return block
    if k == 1:
        return block + 1 - 2 * (block % 2)
    if k == 2:
        return block + 2 - 4 * (block // 2)
    return 3 - block


def project_kernel(
    rows_ref,
    weight_ref,
    kv_ref,
    bias_ref,
    queries_ref,
    keyval_ref,
    asked_ref,
    weight,
    kv,
    feats,
    visual,
    sums,
    got_rep,
    half_sums,
    got_head,
    own_sums,
    got_blk,
    got_queries,
    local_sem,
    feat_send,
    feat_recv,
    sum_send,
    sum_recv,
    query_send,
    query_recv,
):
    block = lax.axis_index("blk")
    head = lax.axis_index("head")
    rep = lax.axis_index("rep")
    rows, depth = feats.shape[1:]
    half = rows // 2
    quarter = rows // 4
    cols = kv.shape[1]
    half_cols = cols // 2
    to_head = {"head": 1 - head}
    to_rep = {"rep": 1 - rep}

    def to_blk(k):
        return {"blk": partner(block, k)}

    def remote(src, dst, send, recv, device):
        return pltpu.make_async_remote_copy(
            src_ref=src,
            dst_ref=dst,
            send_sem=send,
            recv_sem=recv,
            device_id=device,
            device_id_type=pl.DeviceIdType.MESH,
        )

    def quarter_rows(h, r):
        return pl.ds(pl.multiple_of((h * 2 + r) * quarter, quarter), quarter)

    own_rows = quarter_rows(head, rep)
    over_head_rows = quarter_rows(1 - head, rep)

    def feature_columns(k):
        return pl.ds(pl.multiple_of(partner(block, k) * depth, depth), depth)

    load_rows = pltpu.make_async_copy(
        rows_ref.at[:, feature_columns(0)], feats.at[0], local_sem.at[0]
    )
    load_weight = pltpu.make_async_copy(weight_ref, weight, local_sem.at[1])
    load_kv = pltpu.make_async_copy(kv_ref, kv, local_sem.at[2])
    load_rows.start()
    load_weight.start()
    load_kv.start()

    barrier = pltpu.get_barrier_semaphore()
    for device in (to_blk(1), to_blk(2), to_blk(3), to_head, to_rep):
        pl.semaphore_signal(
            barrier, inc=1, device_id=device, device_id_type=pl.DeviceIdType.MESH
        )
    pl.semaphore_wait(barrier, 5)

    started = []

    def begin(copy):
        copy.start()
        started.append(copy)
        return copy

    over_blk = {}
    for k in ORDER[1:]:
        over_blk[k] = begin(
            remote(
                rows_ref.at[own_rows, feature_columns(k)],
                feats.at[k, own_rows],
                feat_send.at[0, k],
                feat_recv.at[0, k],
                to_blk(k),
            )
        )
    asked = [
        begin(
            remote(
                queries_ref, got_queries.at[k], query_send.at[k], query_recv.at[k], to_blk(k)
            )
        )
        for k in (1, 2, 3)
    ]

    over_head, over_rep, last_rep = {}, {}, {}

    def pass_quarter(k):
        over_blk[k].wait_recv()
        piece = feats.at[k, own_rows]
        over_head[k] = begin(
            remote(piece, piece, feat_send.at[1, k], feat_recv.at[1, k], to_head)
        )
        over_rep[k] = begin(
            remote(piece, piece, feat_send.at[2, k], feat_recv.at[2, k], to_rep)
        )

    def pass_second(k):
        over_head[k].wait_recv()
        piece = feats.at[k, over_head_rows]
        last_rep[k] = begin(
            remote(piece, piece, feat_send.at[3, k], feat_recv.at[3, k], to_rep)
        )

    def have_rows(k):
        over_rep[k].wait_recv()
        last_rep[k].wait_recv()

    def multiply(k):
        @pl.loop(0, weight.shape[1] // TILE)
        def _(i):
            at = pl.ds(pl.multiple_of(i * TILE, TILE), TILE)
            visual[:, at] = jnp.dot(
                feats[k], weight[:, at], preferred_element_type=jnp.float32
            ).astype(jnp.bfloat16)

        if k == 0:
            load_kv.wait()

        @pl.loop(0, cols // TILE)
        def _(i):
            at = pl.ds(pl.multiple_of(i * TILE, TILE), TILE)
            sums[k, :, at] = jnp.dot(
                visual[...], kv[:, at], preferred_element_type=jnp.float32
            ).astype(jnp.bfloat16)

    own_half = pl.ds(pl.multiple_of(rep * half, half), half)
    other_half = pl.ds(pl.multiple_of((1 - rep) * half, half), half)
    own_cols = pl.ds(pl.multiple_of(head * half_cols, half_cols), half_cols)
    other_cols = pl.ds(pl.multiple_of((1 - head) * half_cols, half_cols), half_cols)
    by_rep, by_head, by_blk = {}, {}, {}

    def send_rep(k):
        by_rep[k] = begin(
            remote(
                sums.at[k, other_half],
                got_rep.at[k],
                sum_send.at[0, k],
                sum_recv.at[0, k],
                to_rep,
            )
        )

    def send_head(k):
        by_rep[k].wait_recv()
        half_sums[k] = (
            sums[k, own_half, :].astype(jnp.float32) + got_rep[k].astype(jnp.float32)
        ).astype(jnp.bfloat16)
        by_head[k] = begin(
            remote(
                half_sums.at[k, :, other_cols],
                got_head.at[k],
                sum_send.at[1, k],
                sum_recv.at[1, k],
                to_head,
            )
        )

    def send_blk(k):
        by_head[k].wait_recv()
        own_sums[k] = (
            half_sums[k, :, own_cols].astype(jnp.float32) + got_head[k].astype(jnp.float32)
        ).astype(jnp.bfloat16)
        if k != 0:
            by_blk[k] = begin(
                remote(
                    own_sums.at[k],
                    got_blk.at[k],
                    sum_send.at[2, k],
                    sum_recv.at[2, k],
                    to_blk(k),
                )
            )

    first, second, third, fourth = ORDER
    load_rows.wait()
    load_weight.wait()
    multiply(first)
    send_rep(first)
    pass_quarter(second)
    pass_second(second)
    send_head(first)
    pass_quarter(third)
    have_rows(second)
    multiply(second)
    send_rep(second)
    pass_second(third)
    send_head(second)
    send_blk(first)
    pass_quarter(fourth)
    have_rows(third)
    multiply(third)
    send_rep(third)
    pass_second(fourth)
    send_head(third)
    send_blk(second)
    have_rows(fourth)
    multiply(fourth)
    send_rep(fourth)
    send_blk(third)
    send_head(fourth)
    send_blk(fourth)

    asked_ref[block] = queries_ref[...]
    for k in (1, 2, 3):
        asked[k - 1].wait_recv()
        asked_ref[partner(block, k)] = got_queries[k]
    total = own_sums[0].astype(jnp.float32) + bias_ref[...]
    for k in ORDER[1:]:
        by_blk[k].wait_recv()
        total = total + got_blk[k].astype(jnp.float32)
    keyval_ref[...] = total.astype(jnp.bfloat16)
    for copy in started:
        copy.wait_send()


def project_and_ask(merger_rows, out_weight, kv_weight, bias, queries):
    rows = merger_rows.shape[0]
    depth, inner = out_weight.shape
    cols = kv_weight.shape[1]
    half, half_cols = rows // 2, cols // 2
    ask_rows, ask_cols = queries.shape
    kept = jnp.bfloat16
    macs = 4 * rows * inner * (depth + cols)
    hbm = pl.BlockSpec(memory_space=pl.ANY)
    vmem = pl.BlockSpec(memory_space=pltpu.VMEM)
    return pl.pallas_call(
        project_kernel,
        out_shape=(
            jax.ShapeDtypeStruct((half, half_cols), kept),
            jax.ShapeDtypeStruct((4, ask_rows, ask_cols), kept),
        ),
        in_specs=[hbm, hbm, hbm, vmem, vmem],
        out_specs=(vmem, vmem),
        scratch_shapes=[
            pltpu.VMEM((depth, inner), kept),
            pltpu.VMEM((inner, cols), kept),
            pltpu.VMEM((4, rows, depth), kept),
            pltpu.VMEM((rows, inner), kept),
            pltpu.VMEM((4, rows, cols), kept),
            pltpu.VMEM((4, half, cols), kept),
            pltpu.VMEM((4, half, cols), kept),
            pltpu.VMEM((4, half, half_cols), kept),
            pltpu.VMEM((4, half, half_cols), kept),
            pltpu.VMEM((4, half, half_cols), kept),
            pltpu.VMEM((4, ask_rows, ask_cols), kept),
            pltpu.SemaphoreType.DMA((3,)),
            pltpu.SemaphoreType.DMA((4, 4)),
            pltpu.SemaphoreType.DMA((4, 4)),
            pltpu.SemaphoreType.DMA((3, 4)),
            pltpu.SemaphoreType.DMA((3, 4)),
            pltpu.SemaphoreType.DMA((4,)),
            pltpu.SemaphoreType.DMA((4,)),
        ],
        compiler_params=pltpu.CompilerParams(
            collective_id=0, has_side_effects=True, vmem_limit_bytes=VMEM_BYTES
        ),
        cost_estimate=pl.CostEstimate(
            flops=2 * macs,
            bytes_accessed=2 * (rows * 4 * depth + depth * inner + inner * cols),
            transcendentals=0,
        ),
    )(merger_rows, out_weight, kv_weight, bias, queries)


def tiles_fit(merger_rows, out_weight, kv_weight, blocks, head_groups, copies):
    return (
        blocks == 4
        and head_groups == 2
        and copies == 2
        and merger_rows.shape[0] % 64 == 0
        and out_weight.shape[0] % 128 == 0
        and out_weight.shape[1] % TILE == 0
        and kv_weight.shape[1] % TILE == 0
    )


def body(
    merger_rows,
    out_weight,
    kv_weight,
    kv_bias,
    merge_map,
    owner_map,
    old_memory,
    queries,
    retrieved,
):
    blocks = lax.axis_size("blk")
    copies = lax.axis_size("rep")
    head_groups = lax.axis_size("head")
    local_heads = KVH // head_groups
    width = kv_weight.shape[1] // KVH
    head_size = width // 2
    group_index = lax.axis_index("blk") * copies + lax.axis_index("rep")

    bias = kv_bias.reshape(1, -1)
    if tiles_fit(merger_rows, out_weight, kv_weight, blocks, head_groups, copies):
        keyval, asked = project_and_ask(
            merger_rows,
            out_weight,
            kv_weight,
            bias,
            queries.reshape(-1, queries.shape[3]),
        )
        asked = asked.reshape((blocks,) + queries.shape[1:])
    else:
        keyval = project(merger_rows, out_weight, kv_weight, blocks, head_groups, copies)
        keyval = (keyval.astype(jnp.float32) + bias).astype(jnp.bfloat16)
        asked = lax.all_gather(queries, "blk", axis=0, tiled=True)
    half_rows = keyval.shape[0]

    unit_count = half_rows // UNIT_TOK
    capacity = 2 * ((unit_count + blocks - 1) // blocks)
    owners = owner_map[:, 0]
    positions = jnp.arange(unit_count, dtype=jnp.int32)
    same_owner = owners[:, None] == owners[None, :]
    earlier = positions[None, :] < positions[:, None]
    ranks = jnp.sum((same_owner & earlier).astype(jnp.int32), axis=1)
    slots = owners * capacity + ranks
    row_slots = jnp.repeat(slots * UNIT_TOK, UNIT_TOK) + jnp.tile(
        jnp.arange(UNIT_TOK, dtype=jnp.int32), unit_count
    )
    placed_at = merge_map[0][:, None] == jnp.arange(half_rows, dtype=jnp.int32)[None, :]
    row_target = jnp.sum(jnp.where(placed_at, row_slots[:, None], 0), axis=0)
    slot_rows = blocks * capacity * UNIT_TOK
    select = row_target[None, :] == jnp.arange(slot_rows, dtype=jnp.int32)[:, None]
    send = jnp.dot(select.astype(jnp.bfloat16), keyval, preferred_element_type=jnp.float32)
    send = send.astype(jnp.bfloat16).reshape(blocks, capacity * UNIT_TOK, keyval.shape[1])
    arrived = lax.all_to_all(send, "blk", split_axis=0, concat_axis=0, tiled=True)
    new_memory = arrived.reshape(blocks * capacity, UNIT_TOK, local_heads, width)

    old_count = old_memory.shape[0]
    old_ids = group_index * old_count + jnp.arange(old_count, dtype=jnp.int32)
    new_ids = old_count * blocks * copies + group_index * unit_count + positions
    old_listed = jnp.any(retrieved[:, :, None] == old_ids[None, None, :], axis=1)
    new_listed = jnp.any(retrieved[:, :, None] == new_ids[None, None, :], axis=1)
    slot_listed = jnp.repeat(new_listed, UNIT_TOK, axis=1)
    row_listed = jnp.any(slot_listed[:, :, None] & placed_at[None], axis=1)
    mask = jnp.concatenate([jnp.repeat(old_listed, UNIT_TOK, axis=1), row_listed], axis=1)

    query_rows = queries.shape[1]
    per_head = queries.shape[3] // head_size
    slice_rows = query_rows // copies
    questions = asked.shape[0]
    asked = asked.reshape(questions, query_rows, local_heads, per_head, head_size)
    old_flat = old_memory.reshape(-1, local_heads, width)
    flat = jnp.concatenate([old_flat, keyval.reshape(half_rows, local_heads, width)], axis=0)
    keys = flat[..., :head_size]
    values = flat[..., head_size:]
    wide_mask = mask[None, :, None, None, :]
    scores = jnp.einsum("aqkhd,tkd->kaqht", asked, keys, preferred_element_type=jnp.float32)
    scores = jnp.where(wide_mask, scores * head_size ** (-0.5), -1e30)
    peak = jnp.max(scores, axis=-1)
    weights = jnp.where(wide_mask, jnp.exp(scores - peak[..., None]), 0.0)
    total = jnp.sum(weights, axis=-1)
    output = jnp.einsum(
        "kaqht,tkd->kaqhd", weights.astype(jnp.bfloat16), values, preferred_element_type=jnp.float32
    )

    def by_holder(part):
        part = part.reshape((local_heads, questions, copies, slice_rows) + part.shape[3:])
        part = jnp.moveaxis(part, 0, 3)
        return part.reshape((questions * copies, slice_rows * local_heads * per_head) + part.shape[5:])

    answer_rows = slice_rows * local_heads * per_head
    stat_rows = -(-answer_rows // head_size)
    spare = ((0, 0), (0, stat_rows * head_size - answer_rows))
    stats = jnp.stack([jnp.pad(by_holder(peak), spare), jnp.pad(by_holder(total), spare)], axis=1)
    partial = jnp.concatenate(
        [by_holder(output), stats.reshape(questions * copies, 2 * stat_rows, head_size)], axis=1
    )
    partial = lax.all_to_all(partial, ("blk", "rep"), split_axis=0, concat_axis=0, tiled=True)
    outputs = partial[:, :answer_rows]
    stats = partial[:, answer_rows:].reshape(-1, 2, stat_rows * head_size)[..., :answer_rows]
    scale = jnp.exp(stats[:, 0] - jnp.max(stats[:, 0], axis=0, keepdims=True))
    total = jnp.sum(stats[:, 1] * scale, axis=0)
    result = jnp.sum(outputs * scale[..., None], axis=0) / total[:, None]
    answer = result.reshape(1, slice_rows, local_heads, per_head * head_size).astype(jnp.bfloat16)
    return (answer, new_memory)


def solution(mesh):
    placed = (
        P(("groups", "blk"), None),
        P("blk", ("head", "rep")),
        P(("head", "rep"), None),
        P("head", None),
        P(("groups", "blk", "rep"), None),
        P(("groups", "blk", "rep"), None),
        P(("groups", "blk", "rep"), None, "head", None),
        P(("groups", "blk"), None, "head", None),
        P("groups", None),
    )
    return jax.shard_map(
        body,
        mesh=mesh,
        in_specs=placed,
        out_specs=(
            P(("groups", "blk"), "rep", "head", None),
            P(("groups", "blk", "rep"), None, "head", None),
        ),
        check_vma=False,
    )
```

```python
import jax
import jax.numpy as jnp
from jax import lax
from jax.experimental import pallas as pl
from jax.experimental.pallas import tpu as pltpu
from jax.sharding import PartitionSpec as P

KVH = 8
UNIT_TOK = 8


def project(merger_rows, out_weight, kv_weight, blocks, head_groups, copies):
    rows = merger_rows.shape[0]
    depth = out_weight.shape[0]
    split = merger_rows.reshape(rows, blocks, depth).transpose(1, 0, 2)
    features = lax.all_to_all(split, "blk", split_axis=0, concat_axis=0, tiled=True)
    visual = jnp.dot(
        features.reshape(blocks * rows, depth), out_weight, preferred_element_type=jnp.float32
    ).astype(jnp.bfloat16)
    partial = jnp.dot(visual, kv_weight, preferred_element_type=jnp.float32).astype(jnp.bfloat16)
    cols = kv_weight.shape[1] // head_groups
    partial = partial.reshape(blocks, copies, rows // copies, head_groups, cols)
    partial = partial.transpose(0, 3, 1, 2, 4).reshape(-1, rows // copies, cols)
    return lax.psum_scatter(
        partial, ("blk", "head", "rep"), scatter_dimension=0, tiled=True
    ).reshape(rows // copies, cols)


TILE = 512
ORDER = (0, 2, 3, 1)
VMEM_BYTES = 48 * 1024 * 1024


def partner(block, k):
    if k == 0:
        return block
    if k == 1:
        return block + 1 - 2 * (block % 2)
    if k == 2:
        return block + 2 - 4 * (block // 2)
    return 3 - block


def project_kernel(
    rows_ref,
    weight_ref,
    kv_ref,
    bias_ref,
    queries_ref,
    stored_ref,
    retrieved_ref,
    merge_ref,
    owner_ref,
    answer_ref,
    memory_ref,
    weight,
    kv,
    feats,
    visual,
    sums,
    got_rep,
    half_sums,
    got_head,
    own_sums,
    got_blk,
    asked,
    stored,
    old_out,
    old_out_send,
    old_out_got,
    old_log,
    old_log_send,
    old_log_got,
    new_rows,
    new_mask,
    units,
    got_units,
    out_send,
    out_got,
    log_full,
    log_send,
    log_got,
    local_sem,
    feat_send,
    feat_recv,
    sum_send,
    sum_recv,
    query_send,
    query_recv,
    rep_send,
    rep_recv,
    end_send,
    end_recv,
):
    block = lax.axis_index("blk")
    head = lax.axis_index("head")
    rep = lax.axis_index("rep")
    rows, depth = feats.shape[1:]
    half = rows // 2
    quarter = rows // 4
    cols = kv.shape[1]
    half_cols = cols // 2
    to_head = {"head": 1 - head}
    to_rep = {"rep": 1 - rep}

    def to_blk(k):
        return {"blk": partner(block, k)}

    def remote(src, dst, send, recv, device):
        return pltpu.make_async_remote_copy(
            src_ref=src,
            dst_ref=dst,
            send_sem=send,
            recv_sem=recv,
            device_id=device,
            device_id_type=pl.DeviceIdType.MESH,
        )

    def quarter_rows(h, r):
        return pl.ds(pl.multiple_of((h * 2 + r) * quarter, quarter), quarter)

    own_rows = quarter_rows(head, rep)
    over_head_rows = quarter_rows(1 - head, rep)

    def feature_columns(k):
        return pl.ds(pl.multiple_of(partner(block, k) * depth, depth), depth)

    load_rows = pltpu.make_async_copy(
        rows_ref.at[:, feature_columns(0)], feats.at[0], local_sem.at[0]
    )
    load_weight = pltpu.make_async_copy(weight_ref, weight, local_sem.at[1])
    load_kv = pltpu.make_async_copy(kv_ref, kv, local_sem.at[2])
    load_rows.start()
    load_weight.start()
    load_kv.start()
    load_stored = pltpu.make_async_copy(stored_ref, stored, local_sem.at[3])
    load_stored.start()

    barrier = pltpu.get_barrier_semaphore()
    for device in (to_blk(1), to_blk(2), to_blk(3), to_head, to_rep):
        pl.semaphore_signal(
            barrier, inc=1, device_id=device, device_id_type=pl.DeviceIdType.MESH
        )
    pl.semaphore_wait(barrier, 5)

    started = []

    def begin(copy):
        copy.start()
        started.append(copy)
        return copy

    asking = [
        begin(
            remote(queries_ref, asked.at[k], query_send.at[k], query_recv.at[k], to_blk(k))
        )
        for k in (1, 2, 3)
    ]
    over_blk = {}
    for k in ORDER[1:]:
        over_blk[k] = begin(
            remote(
                rows_ref.at[own_rows, feature_columns(k)],
                feats.at[k, own_rows],
                feat_send.at[0, k],
                feat_recv.at[0, k],
                to_blk(k),
            )
        )

    over_head, over_rep, last_rep = {}, {}, {}

    def pass_quarter(k):
        over_blk[k].wait_recv()
        piece = feats.at[k, own_rows]
        over_head[k] = begin(
            remote(piece, piece, feat_send.at[1, k], feat_recv.at[1, k], to_head)
        )
        over_rep[k] = begin(
            remote(piece, piece, feat_send.at[2, k], feat_recv.at[2, k], to_rep)
        )

    def pass_second(k):
        over_head[k].wait_recv()
        piece = feats.at[k, over_head_rows]
        last_rep[k] = begin(
            remote(piece, piece, feat_send.at[3, k], feat_recv.at[3, k], to_rep)
        )

    def have_rows(k):
        over_rep[k].wait_recv()
        last_rep[k].wait_recv()

    def multiply(k):
        @pl.loop(0, weight.shape[1] // TILE)
        def _(i):
            at = pl.ds(pl.multiple_of(i * TILE, TILE), TILE)
            visual[:, at] = jnp.dot(
                feats[k], weight[:, at], preferred_element_type=jnp.float32
            ).astype(jnp.bfloat16)

        if k == 0:
            load_kv.wait()

        @pl.loop(0, cols // TILE)
        def _(i):
            at = pl.ds(pl.multiple_of(i * TILE, TILE), TILE)
            sums[k, :, at] = jnp.dot(
                visual[...], kv[:, at], preferred_element_type=jnp.float32
            ).astype(jnp.bfloat16)

    own_half = pl.ds(pl.multiple_of(rep * half, half), half)
    other_half = pl.ds(pl.multiple_of((1 - rep) * half, half), half)
    own_cols = pl.ds(pl.multiple_of(head * half_cols, half_cols), half_cols)
    other_cols = pl.ds(pl.multiple_of((1 - head) * half_cols, half_cols), half_cols)
    by_rep, by_head, by_blk = {}, {}, {}

    def send_rep(k):
        by_rep[k] = begin(
            remote(
                sums.at[k, other_half],
                got_rep.at[k],
                sum_send.at[0, k],
                sum_recv.at[0, k],
                to_rep,
            )
        )

    def send_head(k):
        by_rep[k].wait_recv()
        half_sums[k] = (
            sums[k, own_half, :].astype(jnp.float32) + got_rep[k].astype(jnp.float32)
        ).astype(jnp.bfloat16)
        by_head[k] = begin(
            remote(
                half_sums.at[k, :, other_cols],
                got_head.at[k],
                sum_send.at[1, k],
                sum_recv.at[1, k],
                to_head,
            )
        )

    def send_blk(k):
        by_head[k].wait_recv()
        own_sums[k] = (
            half_sums[k, :, own_cols].astype(jnp.float32) + got_head[k].astype(jnp.float32)
        ).astype(jnp.bfloat16)
        if k != 0:
            by_blk[k] = begin(
                remote(
                    own_sums.at[k],
                    got_blk.at[k],
                    sum_send.at[2, k],
                    sum_recv.at[2, k],
                    to_blk(k),
                )
            )

    heads = stored.shape[0]
    stored_rows = stored.shape[1]
    head_size = asked.shape[3]
    ask_rows = asked.shape[2] // heads
    group = asked.shape[2]
    new_count = half // UNIT_TOK
    scale = head_size ** (-0.5)
    place = block * 2 + rep
    floats = jnp.float32

    def iota(shape, dim):
        return lax.broadcasted_iota(jnp.int32, shape, dim)

    def listed(ids):
        units_of = jnp.concatenate(
            [retrieved_ref[pl.ds(partner(block, k), 1), :] for k in range(4)], axis=0
        )
        hit = jnp.zeros((4, ids.shape[1]), floats)
        for j in range(units_of.shape[1]):
            hit = jnp.where(ids == units_of[:, j : j + 1], 1.0, hit)
        return hit

    def row_mask(mask, count):
        return jnp.concatenate(
            [
                jnp.broadcast_to(mask[k : k + 1], (count, mask.shape[1]))
                for k in range(4)
            ],
            axis=0,
        )

    def flat_log(wide):
        return jnp.transpose(wide)[:8]

    def wide_log(flat):
        return jnp.transpose(jnp.broadcast_to(flat[:1], (group, group)))

    def prepare():
        eye = iota((new_count, new_count), 0) == iota((new_count, new_count), 1)
        owner = owner_ref[...].astype(floats)
        owner_row = jnp.sum(jnp.where(eye, owner, 0.0), axis=0, keepdims=True)
        earlier = iota((new_count, new_count), 1) < iota((new_count, new_count), 0)
        rank = jnp.sum(
            jnp.where((owner == owner_row) & earlier, 1.0, 0.0), axis=1, keepdims=True
        )
        capacity = units.shape[1] // UNIT_TOK
        slot = owner * capacity + rank
        slot_row = jnp.sum(jnp.where(eye, slot, 0.0), axis=0, keepdims=True)
        of_unit = iota((half, new_count), 0) // UNIT_TOK == iota((half, new_count), 1)
        slot_of = jnp.sum(jnp.where(of_unit, slot_row, 0.0), axis=1, keepdims=True)
        position = iota((half, 1), 0)
        target = slot_of * UNIT_TOK + (position % UNIT_TOK).astype(floats)
        fills = merge_ref[...] == iota((half, half), 1)
        target_row = jnp.sum(jnp.where(fills, target, 0.0), axis=0, keepdims=True)
        unit_of = (position // UNIT_TOK).astype(floats)
        unit_row = jnp.sum(jnp.where(fills, unit_of, 0.0), axis=0, keepdims=True)
        slots = units.shape[0] * units.shape[1]
        select = jnp.where(
            iota((slots, half), 0) == target_row.astype(jnp.int32), 1.0, 0.0
        ).astype(jnp.bfloat16)
        base = stored_rows // UNIT_TOK * 8 + place * new_count
        new_mask[0] = jnp.zeros(new_mask.shape[1:], floats)
        new_mask[0, 0:4, 0:half] = listed(base + unit_row.astype(jnp.int32))
        return select

    def attend_stored():
        ids = place * (stored_rows // UNIT_TOK) + iota((1, stored_rows), 1) // UNIT_TOK
        mask = row_mask(listed(ids), 2 * ask_rows) > 0.0

        @pl.loop(0, heads)
        def _(h):
            at = pl.ds(pl.multiple_of(h * ask_rows, ask_rows), ask_rows)
            query = jnp.concatenate(
                [asked[k, r, at, :] for k in range(4) for r in range(2)], axis=0
            )
            scores = lax.dot_general(
                query,
                stored[h, :, :head_size],
                (((1,), (1,)), ((), ())),
                preferred_element_type=floats,
            )
            scores = jnp.where(mask, scores * scale, -1e30)
            peak = jnp.max(scores, axis=1, keepdims=True)
            weights = jnp.where(mask, jnp.exp(scores - peak), 0.0)
            total = jnp.maximum(jnp.sum(weights, axis=1, keepdims=True), 1e-30)
            output = jnp.dot(
                weights.astype(jnp.bfloat16),
                stored[h, :, head_size:],
                preferred_element_type=floats,
            )
            output = output / total
            logs = jnp.broadcast_to(peak + jnp.log(total), output.shape)
            for k in range(4):
                for r in range(2):
                    start = (2 * k + r) * ask_rows
                    old_out[r, k, at, :] = output[start : start + ask_rows]
                    old_log[r, k, at, :] = logs[start : start + ask_rows]

        old_out_send[...] = old_out[1 - rep].astype(jnp.bfloat16)
        for k in range(4):
            old_log_send[k] = flat_log(old_log[1 - rep, k])

    old_parts = []

    def send_stored():
        for i, (src, dst) in enumerate(
            (
                (old_out_send, old_out_got),
                (old_log_send, old_log_got),
                (new_mask.at[0], new_mask.at[1]),
            )
        ):
            old_parts.append(
                begin(remote(src, dst, rep_send.at[i], rep_recv.at[i], to_rep))
            )

    def merge_stored():
        for copy in old_parts:
            copy.wait_recv()
        for k in range(4):
            mine, theirs = old_log[rep, k], wide_log(old_log_got[k])
            peak = jnp.maximum(mine, theirs)
            first_part, second_part = jnp.exp(mine - peak), jnp.exp(theirs - peak)
            total = first_part + second_part
            old_out[rep, k] = (
                first_part * old_out[rep, k] + second_part * old_out_got[k].astype(floats)
            ) / total
            old_log[rep, k] = peak + jnp.log(total)

    def attend_new():
        masks = [row_mask(new_mask[i, 0:4, 0:half], ask_rows) > 0.0 for i in range(2)]

        @pl.loop(0, heads)
        def _(h):
            at = pl.ds(pl.multiple_of(h * ask_rows, ask_rows), ask_rows)
            key_at = pl.ds(pl.multiple_of(h * 2 * head_size, head_size), head_size)
            value_at = pl.ds(
                pl.multiple_of(h * 2 * head_size + head_size, head_size), head_size
            )
            query = jnp.concatenate([asked[k, rep, at, :] for k in range(4)], axis=0)
            before = jnp.concatenate([old_log[rep, k, at, :] for k in range(4)], axis=0)
            output = jnp.concatenate([old_out[rep, k, at, :] for k in range(4)], axis=0)
            peak, scores = before, []
            for i in range(2):
                part = lax.dot_general(
                    query,
                    new_rows[i, :, key_at],
                    (((1,), (1,)), ((), ())),
                    preferred_element_type=floats,
                )
                part = jnp.where(masks[i], part * scale, -1e30)
                scores.append(part)
                peak = jnp.maximum(peak, jnp.max(part, axis=1, keepdims=True))
            total = jnp.exp(before - peak)
            output = output * total
            for i in range(2):
                weights = jnp.where(masks[i], jnp.exp(scores[i] - peak[:, :half]), 0.0)
                total = total + jnp.sum(weights, axis=1, keepdims=True)
                output = output + jnp.dot(
                    weights.astype(jnp.bfloat16),
                    new_rows[i, :, value_at],
                    preferred_element_type=floats,
                )
            total = jnp.maximum(total, 1e-30)
            output = output / total
            logs = peak + jnp.log(total)
            for k in range(4):
                part = slice(k * ask_rows, (k + 1) * ask_rows)
                out_send[k, at, :] = output[part].astype(jnp.bfloat16)
                log_full[k, at, :] = logs[part]

    first, second, third, fourth = ORDER
    load_rows.wait()
    load_weight.wait()
    multiply(first)
    send_rep(first)
    pass_quarter(second)
    pass_second(second)
    select = prepare()
    asked[0] = queries_ref[...]
    for copy in asking:
        copy.wait_recv()
    load_stored.wait()
    send_head(first)
    pass_quarter(third)
    attend_stored()
    send_stored()
    have_rows(second)
    multiply(second)
    send_rep(second)
    pass_second(third)
    send_head(second)
    send_blk(first)
    pass_quarter(fourth)
    have_rows(third)
    multiply(third)
    send_rep(third)
    pass_second(fourth)
    send_head(third)
    send_blk(second)
    have_rows(fourth)
    multiply(fourth)
    send_rep(fourth)
    send_blk(third)
    send_head(fourth)
    merge_stored()
    send_blk(fourth)

    total = own_sums[0].astype(floats) + bias_ref[...]
    for k in ORDER[1:]:
        by_blk[k].wait_recv()
        total = total + got_blk[k].astype(floats)
    new_rows[0] = total.astype(jnp.bfloat16)
    share = begin(
        remote(new_rows.at[0], new_rows.at[1], rep_send.at[3], rep_recv.at[3], to_rep)
    )
    units[...] = (
        jnp.dot(select, new_rows[0], preferred_element_type=floats)
        .astype(jnp.bfloat16)
        .reshape(units.shape)
    )
    share.wait_recv()
    attend_new()
    ended = []
    for k in ORDER[1:]:
        log_send[k] = flat_log(log_full[k])
        ended.append(
            (
                begin(
                    remote(
                        out_send.at[k],
                        out_got.at[k],
                        end_send.at[0, k],
                        end_recv.at[0, k],
                        to_blk(k),
                    )
                ),
                begin(
                    remote(
                        log_send.at[k],
                        log_got.at[k],
                        end_send.at[1, k],
                        end_recv.at[1, k],
                        to_blk(k),
                    )
                ),
            )
        )
    relayout = []
    for k in ORDER[1:]:
        relayout.append(
            begin(
                remote(
                    units.at[partner(block, k)],
                    got_units.at[k],
                    end_send.at[2, k],
                    end_recv.at[2, k],
                    to_blk(k),
                )
            )
        )
    memory_ref[block] = units[block]
    logs = [log_full[0]]
    outputs = [out_send[0].astype(floats)]
    for k, copies in zip(ORDER[1:], ended):
        for copy in copies:
            copy.wait_recv()
        logs.append(wide_log(log_got[k]))
        outputs.append(out_got[k].astype(floats))
    peak = jnp.maximum(jnp.maximum(logs[0], logs[1]), jnp.maximum(logs[2], logs[3]))
    parts = [jnp.exp(one - peak) for one in logs]
    mixed = sum(part * output for part, output in zip(parts, outputs))
    answer_ref[...] = (mixed / sum(parts)).astype(jnp.bfloat16)
    for k, copy in zip(ORDER[1:], relayout):
        copy.wait_recv()
        memory_ref[partner(block, k)] = got_units[k]
    for copy in started:
        copy.wait_send()


def whole_step(
    merger_rows, out_weight, kv_weight, bias, queries, stored, retrieved, merge_map, owner_map
):
    rows = merger_rows.shape[0]
    depth, inner = out_weight.shape
    cols = kv_weight.shape[1]
    half, half_cols = rows // 2, cols // 2
    group, head_size = queries.shape[1:]
    new_count = half // UNIT_TOK
    slot_rows = 2 * ((new_count + 3) // 4) * UNIT_TOK
    kept, wide = jnp.bfloat16, jnp.float32
    macs = 4 * rows * inner * (depth + cols)
    hbm = pl.BlockSpec(memory_space=pl.ANY)
    vmem = pl.BlockSpec(memory_space=pltpu.VMEM)
    scratch = [
        ((depth, inner), kept),
        ((inner, cols), kept),
        ((4, rows, depth), kept),
        ((rows, inner), kept),
        ((4, rows, cols), kept),
        ((4, half, cols), kept),
        ((4, half, cols), kept),
        ((4, half, half_cols), kept),
        ((4, half, half_cols), kept),
        ((4, half, half_cols), kept),
        ((4, 2, group, head_size), kept),
        (stored.shape, kept),
        ((2, 4, group, head_size), wide),
        ((4, group, head_size), kept),
        ((4, group, head_size), kept),
        ((2, 4, group, head_size), wide),
        ((4, 8, head_size), wide),
        ((4, 8, head_size), wide),
        ((2, half, half_cols), kept),
        ((2, 8, 128), wide),
        ((4, slot_rows, half_cols), kept),
        ((4, slot_rows, half_cols), kept),
        ((4, group, head_size), kept),
        ((4, group, head_size), kept),
        ((4, group, head_size), wide),
        ((4, 8, head_size), wide),
        ((4, 8, head_size), wide),
    ]
    semaphores = [(4,), (4, 4), (4, 4), (3, 4), (3, 4), (4,), (4,), (4,), (4,), (3, 4), (3, 4)]
    return pl.pallas_call(
        project_kernel,
        out_shape=(
            jax.ShapeDtypeStruct((group, head_size), kept),
            jax.ShapeDtypeStruct((4, slot_rows, half_cols), kept),
        ),
        in_specs=[hbm, hbm, hbm, vmem, vmem, hbm, vmem, vmem, vmem],
        out_specs=(vmem, vmem),
        scratch_shapes=[pltpu.VMEM(shape, kind) for shape, kind in scratch]
        + [pltpu.SemaphoreType.DMA(shape) for shape in semaphores],
        compiler_params=pltpu.CompilerParams(
            collective_id=0, has_side_effects=True, vmem_limit_bytes=VMEM_BYTES
        ),
        cost_estimate=pl.CostEstimate(
            flops=2 * macs,
            bytes_accessed=2 * (rows * 4 * depth + depth * inner + inner * cols),
            transcendentals=0,
        ),
    )(merger_rows, out_weight, kv_weight, bias, queries, stored, retrieved, merge_map, owner_map)


def tiles_fit(
    merger_rows, out_weight, kv_weight, blocks, head_groups, copies, answer_rows, head_size
):
    return (
        blocks == 4
        and head_groups == 2
        and copies == 2
        and merger_rows.shape[0] % 64 == 0
        and out_weight.shape[0] % 128 == 0
        and out_weight.shape[1] % TILE == 0
        and kv_weight.shape[1] % TILE == 0
        and answer_rows == head_size == 128
        and merger_rows.shape[0] // copies <= 128
    )


def body(
    merger_rows,
    out_weight,
    kv_weight,
    kv_bias,
    merge_map,
    owner_map,
    old_memory,
    queries,
    retrieved,
):
    blocks = lax.axis_size("blk")
    copies = lax.axis_size("rep")
    head_groups = lax.axis_size("head")
    local_heads = KVH // head_groups
    width = kv_weight.shape[1] // KVH
    head_size = width // 2
    group_index = lax.axis_index("blk") * copies + lax.axis_index("rep")

    bias = kv_bias.reshape(1, -1)
    query_rows = queries.shape[1]
    per_head = queries.shape[3] // head_size
    slice_rows = query_rows // copies
    answer_rows = slice_rows * local_heads * per_head
    if tiles_fit(
        merger_rows, out_weight, kv_weight, blocks, head_groups, copies, answer_rows, head_size
    ):
        asking = queries.reshape(copies, slice_rows, local_heads, per_head, head_size)
        asking = asking.transpose(0, 2, 1, 3, 4).reshape(copies, answer_rows, head_size)
        stored = old_memory.reshape(-1, local_heads, width).transpose(1, 0, 2)
        answer, new_memory = whole_step(
            merger_rows,
            out_weight,
            kv_weight,
            bias,
            asking,
            stored,
            retrieved,
            merge_map.reshape(-1, 1),
            owner_map,
        )
        answer = answer.reshape(local_heads, slice_rows, per_head * head_size)
        return (
            answer.transpose(1, 0, 2)[None],
            new_memory.reshape(-1, UNIT_TOK, local_heads, width),
        )
    keyval = project(merger_rows, out_weight, kv_weight, blocks, head_groups, copies)
    keyval = (keyval.astype(jnp.float32) + bias).astype(jnp.bfloat16)
    asked = lax.all_gather(queries, "blk", axis=0, tiled=True)
    half_rows = keyval.shape[0]

    unit_count = half_rows // UNIT_TOK
    capacity = 2 * ((unit_count + blocks - 1) // blocks)
    owners = owner_map[:, 0]
    positions = jnp.arange(unit_count, dtype=jnp.int32)
    same_owner = owners[:, None] == owners[None, :]
    earlier = positions[None, :] < positions[:, None]
    ranks = jnp.sum((same_owner & earlier).astype(jnp.int32), axis=1)
    slots = owners * capacity + ranks
    row_slots = jnp.repeat(slots * UNIT_TOK, UNIT_TOK) + jnp.tile(
        jnp.arange(UNIT_TOK, dtype=jnp.int32), unit_count
    )
    placed_at = merge_map[0][:, None] == jnp.arange(half_rows, dtype=jnp.int32)[None, :]
    row_target = jnp.sum(jnp.where(placed_at, row_slots[:, None], 0), axis=0)
    slot_rows = blocks * capacity * UNIT_TOK
    select = row_target[None, :] == jnp.arange(slot_rows, dtype=jnp.int32)[:, None]
    send = jnp.dot(select.astype(jnp.bfloat16), keyval, preferred_element_type=jnp.float32)
    send = send.astype(jnp.bfloat16).reshape(blocks, capacity * UNIT_TOK, keyval.shape[1])
    arrived = lax.all_to_all(send, "blk", split_axis=0, concat_axis=0, tiled=True)
    new_memory = arrived.reshape(blocks * capacity, UNIT_TOK, local_heads, width)

    old_count = old_memory.shape[0]
    old_ids = group_index * old_count + jnp.arange(old_count, dtype=jnp.int32)
    new_ids = old_count * blocks * copies + group_index * unit_count + positions
    old_listed = jnp.any(retrieved[:, :, None] == old_ids[None, None, :], axis=1)
    new_listed = jnp.any(retrieved[:, :, None] == new_ids[None, None, :], axis=1)
    slot_listed = jnp.repeat(new_listed, UNIT_TOK, axis=1)
    row_listed = jnp.any(slot_listed[:, :, None] & placed_at[None], axis=1)
    mask = jnp.concatenate([jnp.repeat(old_listed, UNIT_TOK, axis=1), row_listed], axis=1)

    questions = asked.shape[0]
    asked = asked.reshape(questions, query_rows, local_heads, per_head, head_size)
    old_flat = old_memory.reshape(-1, local_heads, width)
    flat = jnp.concatenate([old_flat, keyval.reshape(half_rows, local_heads, width)], axis=0)
    keys = flat[..., :head_size]
    values = flat[..., head_size:]
    wide_mask = mask[None, :, None, None, :]
    scores = jnp.einsum("aqkhd,tkd->kaqht", asked, keys, preferred_element_type=jnp.float32)
    scores = jnp.where(wide_mask, scores * head_size ** (-0.5), -1e30)
    peak = jnp.max(scores, axis=-1)
    weights = jnp.where(wide_mask, jnp.exp(scores - peak[..., None]), 0.0)
    total = jnp.sum(weights, axis=-1)
    output = jnp.einsum(
        "kaqht,tkd->kaqhd", weights.astype(jnp.bfloat16), values, preferred_element_type=jnp.float32
    )

    def by_holder(part):
        part = part.reshape((local_heads, questions, copies, slice_rows) + part.shape[3:])
        part = jnp.moveaxis(part, 0, 3)
        return part.reshape((questions * copies, slice_rows * local_heads * per_head) + part.shape[5:])

    stat_rows = -(-answer_rows // head_size)
    spare = ((0, 0), (0, stat_rows * head_size - answer_rows))
    stats = jnp.stack([jnp.pad(by_holder(peak), spare), jnp.pad(by_holder(total), spare)], axis=1)
    partial = jnp.concatenate(
        [by_holder(output), stats.reshape(questions * copies, 2 * stat_rows, head_size)], axis=1
    )
    partial = lax.all_to_all(partial, ("blk", "rep"), split_axis=0, concat_axis=0, tiled=True)
    outputs = partial[:, :answer_rows]
    stats = partial[:, answer_rows:].reshape(-1, 2, stat_rows * head_size)[..., :answer_rows]
    scale = jnp.exp(stats[:, 0] - jnp.max(stats[:, 0], axis=0, keepdims=True))
    total = jnp.sum(stats[:, 1] * scale, axis=0)
    result = jnp.sum(outputs * scale[..., None], axis=0) / total[:, None]
    answer = result.reshape(1, slice_rows, local_heads, per_head * head_size).astype(jnp.bfloat16)
    return (answer, new_memory)


def solution(mesh):
    placed = (
        P(("groups", "blk"), None),
        P("blk", ("head", "rep")),
        P(("head", "rep"), None),
        P("head", None),
        P(("groups", "blk", "rep"), None),
        P(("groups", "blk", "rep"), None),
        P(("groups", "blk", "rep"), None, "head", None),
        P(("groups", "blk"), None, "head", None),
        P("groups", None),
    )
    return jax.shard_map(
        body,
        mesh=mesh,
        in_specs=placed,
        out_specs=(
            P(("groups", "blk"), "rep", "head", None),
            P(("groups", "blk", "rep"), None, "head", None),
        ),
        check_vma=False,
    )
```

```python
import jax
import jax.numpy as jnp
from jax import lax
from jax.experimental import pallas as pl
from jax.experimental.pallas import tpu as pltpu
from jax.sharding import PartitionSpec as P

KVH = 8
UNIT_TOK = 8


def project(merger_rows, out_weight, kv_weight, blocks, head_groups, copies):
    rows = merger_rows.shape[0]
    depth = out_weight.shape[0]
    split = merger_rows.reshape(rows, blocks, depth).transpose(1, 0, 2)
    features = lax.all_to_all(split, "blk", split_axis=0, concat_axis=0, tiled=True)
    visual = jnp.dot(
        features.reshape(blocks * rows, depth), out_weight, preferred_element_type=jnp.float32
    ).astype(jnp.bfloat16)
    partial = jnp.dot(visual, kv_weight, preferred_element_type=jnp.float32).astype(jnp.bfloat16)
    cols = kv_weight.shape[1] // head_groups
    partial = partial.reshape(blocks, copies, rows // copies, head_groups, cols)
    partial = partial.transpose(0, 3, 1, 2, 4).reshape(-1, rows // copies, cols)
    return lax.psum_scatter(
        partial, ("blk", "head", "rep"), scatter_dimension=0, tiled=True
    ).reshape(rows // copies, cols)


TILE = 512
ORDER = (0, 3, 2, 1)
VMEM_BYTES = 48 * 1024 * 1024


def partner(block, k):
    if k == 0:
        return block
    if k == 1:
        return block + 1 - 2 * (block % 2)
    if k == 2:
        return block + 2 - 4 * (block // 2)
    return 3 - block


def project_kernel(
    rows_ref,
    weight_ref,
    kv_ref,
    bias_ref,
    queries_ref,
    stored_ref,
    retrieved_ref,
    merge_ref,
    owner_ref,
    answer_ref,
    memory_ref,
    weight,
    kv,
    feats,
    visual,
    sums,
    got_rep,
    half_sums,
    got_head,
    own_sums,
    got_blk,
    asked,
    stored,
    old_out,
    old_out_send,
    old_out_got,
    old_log,
    old_log_send,
    old_log_got,
    new_rows,
    new_mask,
    units,
    got_units,
    out_send,
    out_got,
    log_full,
    log_send,
    log_got,
    local_sem,
    feat_send,
    feat_recv,
    sum_send,
    sum_recv,
    query_send,
    query_recv,
    rep_send,
    rep_recv,
    end_send,
    end_recv,
):
    block = lax.axis_index("blk")
    head = lax.axis_index("head")
    rep = lax.axis_index("rep")
    rows, depth = feats.shape[1:]
    half = rows // 2
    quarter = rows // 4
    cols = kv.shape[1]
    half_cols = cols // 2
    to_head = {"head": 1 - head}
    to_rep = {"rep": 1 - rep}

    def to_blk(k):
        return {"blk": partner(block, k)}

    def remote(src, dst, send, recv, device):
        return pltpu.make_async_remote_copy(
            src_ref=src,
            dst_ref=dst,
            send_sem=send,
            recv_sem=recv,
            device_id=device,
            device_id_type=pl.DeviceIdType.MESH,
        )

    def quarter_rows(h, r):
        return pl.ds(pl.multiple_of((h * 2 + r) * quarter, quarter), quarter)

    own_rows = quarter_rows(head, rep)
    over_head_rows = quarter_rows(1 - head, rep)

    def feature_columns(k):
        return pl.ds(pl.multiple_of(partner(block, k) * depth, depth), depth)

    load_rows = pltpu.make_async_copy(
        rows_ref.at[:, feature_columns(0)], feats.at[0], local_sem.at[0]
    )
    load_weight = pltpu.make_async_copy(weight_ref, weight, local_sem.at[1])
    load_kv = pltpu.make_async_copy(kv_ref, kv, local_sem.at[2])
    load_rows.start()
    load_weight.start()
    load_kv.start()
    load_stored = pltpu.make_async_copy(stored_ref, stored, local_sem.at[3])
    load_stored.start()

    barrier = pltpu.get_barrier_semaphore()
    for device in (to_blk(1), to_blk(2), to_blk(3), to_head, to_rep):
        pl.semaphore_signal(
            barrier, inc=1, device_id=device, device_id_type=pl.DeviceIdType.MESH
        )
    pl.semaphore_wait(barrier, 5)

    started = []

    def begin(copy):
        copy.start()
        started.append(copy)
        return copy

    over_blk, asking, ask_again = {}, {}, {}

    def send_features(k):
        over_blk[k] = begin(
            remote(
                rows_ref.at[own_rows, feature_columns(k)],
                feats.at[k, own_rows],
                feat_send.at[0, k],
                feat_recv.at[0, k],
                to_blk(k),
            )
        )

    def send_queries():
        for k in (1, 2, 3):
            asking[k] = begin(
                remote(
                    queries_ref.at[rep],
                    asked.at[k, rep],
                    query_send.at[0, k],
                    query_recv.at[0, k],
                    to_blk(k),
                )
            )

    def pass_queries():
        for k in (1, 2, 3):
            asking[k].wait_recv()
            piece = asked.at[k, rep]
            ask_again[k] = begin(
                remote(piece, piece, query_send.at[1, k], query_recv.at[1, k], to_rep)
            )

    send_features(ORDER[1])
    send_features(ORDER[2])
    send_features(ORDER[3])

    over_head, over_rep, last_rep = {}, {}, {}

    def pass_quarter(k):
        over_blk[k].wait_recv()
        piece = feats.at[k, own_rows]
        over_head[k] = begin(
            remote(piece, piece, feat_send.at[1, k], feat_recv.at[1, k], to_head)
        )
        over_rep[k] = begin(
            remote(piece, piece, feat_send.at[2, k], feat_recv.at[2, k], to_rep)
        )

    def pass_second(k):
        over_head[k].wait_recv()
        piece = feats.at[k, over_head_rows]
        last_rep[k] = begin(
            remote(piece, piece, feat_send.at[3, k], feat_recv.at[3, k], to_rep)
        )

    def have_rows(k):
        over_rep[k].wait_recv()
        last_rep[k].wait_recv()

    def multiply(k):
        @pl.loop(0, weight.shape[1] // TILE)
        def _(i):
            at = pl.ds(pl.multiple_of(i * TILE, TILE), TILE)
            visual[:, at] = jnp.dot(
                feats[k], weight[:, at], preferred_element_type=jnp.float32
            ).astype(jnp.bfloat16)

        if k == 0:
            send_queries()
            load_kv.wait()

        @pl.loop(0, cols // TILE)
        def _(i):
            at = pl.ds(pl.multiple_of(i * TILE, TILE), TILE)
            sums[k, :, at] = jnp.dot(
                visual[...], kv[:, at], preferred_element_type=jnp.float32
            ).astype(jnp.bfloat16)

    own_half = pl.ds(pl.multiple_of(rep * half, half), half)
    other_half = pl.ds(pl.multiple_of((1 - rep) * half, half), half)
    own_cols = pl.ds(pl.multiple_of(head * half_cols, half_cols), half_cols)
    other_cols = pl.ds(pl.multiple_of((1 - head) * half_cols, half_cols), half_cols)
    by_rep, by_head, by_blk = {}, {}, {}

    def send_rep(k):
        by_rep[k] = begin(
            remote(
                sums.at[k, other_half],
                got_rep.at[k],
                sum_send.at[0, k],
                sum_recv.at[0, k],
                to_rep,
            )
        )

    def send_head(k):
        by_rep[k].wait_recv()
        half_sums[k] = (
            sums[k, own_half, :].astype(jnp.float32) + got_rep[k].astype(jnp.float32)
        ).astype(jnp.bfloat16)
        by_head[k] = begin(
            remote(
                half_sums.at[k, :, other_cols],
                got_head.at[k],
                sum_send.at[1, k],
                sum_recv.at[1, k],
                to_head,
            )
        )

    def send_blk(k):
        by_head[k].wait_recv()
        own_sums[k] = (
            half_sums[k, :, own_cols].astype(jnp.float32) + got_head[k].astype(jnp.float32)
        ).astype(jnp.bfloat16)
        if k == 0:
            return
        if k == 2:
            by_blk[3].wait_recv()
            own_sums[2] = (
                own_sums[2].astype(jnp.float32) + got_blk[3].astype(jnp.float32)
            ).astype(jnp.bfloat16)
        by_blk[k] = begin(
            remote(
                own_sums.at[k],
                got_blk.at[k],
                sum_send.at[2, k],
                sum_recv.at[2, k],
                to_blk(2 if k == 2 else 1),
            )
        )

    heads = stored.shape[0]
    stored_rows = stored.shape[1]
    head_size = asked.shape[3]
    ask_rows = asked.shape[2] // heads
    group = asked.shape[2]
    new_count = half // UNIT_TOK
    scale = head_size ** (-0.5)
    place = block * 2 + rep
    floats = jnp.float32

    def iota(shape, dim):
        return lax.broadcasted_iota(jnp.int32, shape, dim)

    def listed(ids):
        units_of = jnp.concatenate(
            [retrieved_ref[pl.ds(partner(block, k), 1), :] for k in range(4)], axis=0
        )
        hit = jnp.zeros((4, ids.shape[1]), floats)
        for j in range(units_of.shape[1]):
            hit = jnp.where(ids == units_of[:, j : j + 1], 1.0, hit)
        return hit

    def row_mask(mask, count):
        return jnp.concatenate(
            [
                jnp.broadcast_to(mask[k : k + 1], (count, mask.shape[1]))
                for k in range(4)
            ],
            axis=0,
        )

    def flat_log(wide):
        return jnp.transpose(wide)[:8]

    def wide_log(flat):
        return jnp.transpose(jnp.broadcast_to(flat[:1], (group, group)))

    def prepare():
        eye = iota((new_count, new_count), 0) == iota((new_count, new_count), 1)
        owner = owner_ref[...].astype(floats)
        owner_row = jnp.sum(jnp.where(eye, owner, 0.0), axis=0, keepdims=True)
        earlier = iota((new_count, new_count), 1) < iota((new_count, new_count), 0)
        rank = jnp.sum(
            jnp.where((owner == owner_row) & earlier, 1.0, 0.0), axis=1, keepdims=True
        )
        capacity = units.shape[1] // UNIT_TOK
        slot = owner * capacity + rank
        slot_row = jnp.sum(jnp.where(eye, slot, 0.0), axis=0, keepdims=True)
        of_unit = iota((half, new_count), 0) // UNIT_TOK == iota((half, new_count), 1)
        slot_of = jnp.sum(jnp.where(of_unit, slot_row, 0.0), axis=1, keepdims=True)
        position = iota((half, 1), 0)
        target = slot_of * UNIT_TOK + (position % UNIT_TOK).astype(floats)
        fills = merge_ref[...] == iota((half, half), 1)
        target_row = jnp.sum(jnp.where(fills, target, 0.0), axis=0, keepdims=True)
        unit_of = (position // UNIT_TOK).astype(floats)
        unit_row = jnp.sum(jnp.where(fills, unit_of, 0.0), axis=0, keepdims=True)
        slots = units.shape[0] * units.shape[1]
        select = jnp.where(
            iota((slots, half), 0) == target_row.astype(jnp.int32), 1.0, 0.0
        ).astype(jnp.bfloat16)
        base = stored_rows // UNIT_TOK * 8 + place * new_count
        new_mask[0] = jnp.zeros(new_mask.shape[1:], floats)
        new_mask[0, 0:4, 0:half] = listed(base + unit_row.astype(jnp.int32))
        return select

    def attend_stored():
        ids = place * (stored_rows // UNIT_TOK) + iota((1, stored_rows), 1) // UNIT_TOK
        mask = row_mask(listed(ids), 2 * ask_rows) > 0.0

        @pl.loop(0, heads)
        def _(h):
            at = pl.ds(pl.multiple_of(h * ask_rows, ask_rows), ask_rows)
            query = jnp.concatenate(
                [asked[k, r, at, :] for k in range(4) for r in range(2)], axis=0
            )
            scores = lax.dot_general(
                query,
                stored[h, :, :head_size],
                (((1,), (1,)), ((), ())),
                preferred_element_type=floats,
            )
            scores = jnp.where(mask, scores * scale, -1e30)
            peak = jnp.max(scores, axis=1, keepdims=True)
            weights = jnp.where(mask, jnp.exp(scores - peak), 0.0)
            total = jnp.maximum(jnp.sum(weights, axis=1, keepdims=True), 1e-30)
            output = jnp.dot(
                weights.astype(jnp.bfloat16),
                stored[h, :, head_size:],
                preferred_element_type=floats,
            )
            output = output / total
            logs = jnp.broadcast_to(peak + jnp.log(total), output.shape)
            for k in range(4):
                for r in range(2):
                    start = (2 * k + r) * ask_rows
                    old_out[r, k, at, :] = output[start : start + ask_rows]
                    old_log[r, k, at, :] = logs[start : start + ask_rows]

        old_out_send[...] = old_out[1 - rep].astype(jnp.bfloat16)
        for k in range(4):
            old_log_send[k] = flat_log(old_log[1 - rep, k])

    old_parts = []

    def send_stored():
        for i, (src, dst) in enumerate(
            (
                (old_out_send, old_out_got),
                (old_log_send, old_log_got),
                (new_mask.at[0], new_mask.at[1]),
            )
        ):
            old_parts.append(
                begin(remote(src, dst, rep_send.at[i], rep_recv.at[i], to_rep))
            )

    def merge_stored():
        for copy in old_parts:
            copy.wait_recv()
        for k in range(4):
            mine, theirs = old_log[rep, k], wide_log(old_log_got[k])
            peak = jnp.maximum(mine, theirs)
            first_part, second_part = jnp.exp(mine - peak), jnp.exp(theirs - peak)
            total = first_part + second_part
            old_out[rep, k] = (
                first_part * old_out[rep, k] + second_part * old_out_got[k].astype(floats)
            ) / total
            old_log[rep, k] = peak + jnp.log(total)

    def attend_new():
        masks = [row_mask(new_mask[i, 0:4, 0:half], ask_rows) > 0.0 for i in range(2)]

        @pl.loop(0, heads)
        def _(h):
            at = pl.ds(pl.multiple_of(h * ask_rows, ask_rows), ask_rows)
            key_at = pl.ds(pl.multiple_of(h * 2 * head_size, head_size), head_size)
            value_at = pl.ds(
                pl.multiple_of(h * 2 * head_size + head_size, head_size), head_size
            )
            query = jnp.concatenate([asked[k, rep, at, :] for k in range(4)], axis=0)
            before = jnp.concatenate([old_log[rep, k, at, :] for k in range(4)], axis=0)
            output = jnp.concatenate([old_out[rep, k, at, :] for k in range(4)], axis=0)
            peak, scores = before, []
            for i in range(2):
                part = lax.dot_general(
                    query,
                    new_rows[i, :, key_at],
                    (((1,), (1,)), ((), ())),
                    preferred_element_type=floats,
                )
                part = jnp.where(masks[i], part * scale, -1e30)
                scores.append(part)
                peak = jnp.maximum(peak, jnp.max(part, axis=1, keepdims=True))
            total = jnp.exp(before - peak)
            output = output * total
            for i in range(2):
                weights = jnp.where(masks[i], jnp.exp(scores[i] - peak[:, :half]), 0.0)
                total = total + jnp.sum(weights, axis=1, keepdims=True)
                output = output + jnp.dot(
                    weights.astype(jnp.bfloat16),
                    new_rows[i, :, value_at],
                    preferred_element_type=floats,
                )
            total = jnp.maximum(total, 1e-30)
            output = output / total
            logs = peak + jnp.log(total)
            for k in range(4):
                part = slice(k * ask_rows, (k + 1) * ask_rows)
                out_send[k, at, :] = output[part].astype(jnp.bfloat16)
                log_full[k, at, :] = logs[part]

    first, second, third, fourth = ORDER
    load_rows.wait()
    load_weight.wait()
    multiply(first)
    send_rep(first)
    pass_quarter(second)
    pass_second(second)
    select = prepare()
    asked[0] = queries_ref[...]
    send_head(first)
    pass_queries()
    pass_quarter(third)
    load_stored.wait()
    for copy in ask_again.values():
        copy.wait_recv()
    attend_stored()
    send_stored()
    have_rows(second)
    multiply(second)
    send_rep(second)
    pass_second(third)
    send_head(second)
    send_blk(first)
    pass_quarter(fourth)
    have_rows(third)
    multiply(third)
    send_rep(third)
    pass_second(fourth)
    send_head(third)
    send_blk(second)
    have_rows(fourth)
    multiply(fourth)
    send_rep(fourth)
    send_blk(third)
    send_head(fourth)
    merge_stored()
    send_blk(fourth)

    total = own_sums[0].astype(floats) + bias_ref[...]
    for k in (2, 1):
        by_blk[k].wait_recv()
        total = total + got_blk[k].astype(floats)
    new_rows[0] = total.astype(jnp.bfloat16)
    share = begin(
        remote(new_rows.at[0], new_rows.at[1], rep_send.at[3], rep_recv.at[3], to_rep)
    )
    units[...] = (
        jnp.dot(select, new_rows[0], preferred_element_type=floats)
        .astype(jnp.bfloat16)
        .reshape(units.shape)
    )
    relayout = []
    for k in ORDER[1:]:
        relayout.append(
            begin(
                remote(
                    units.at[partner(block, k)],
                    got_units.at[k],
                    end_send.at[2, k],
                    end_recv.at[2, k],
                    to_blk(k),
                )
            )
        )
    share.wait_recv()
    attend_new()
    ended = []
    for k in ORDER[1:]:
        log_send[k] = flat_log(log_full[k])
        ended.append(
            (
                begin(
                    remote(
                        out_send.at[k],
                        out_got.at[k],
                        end_send.at[0, k],
                        end_recv.at[0, k],
                        to_blk(k),
                    )
                ),
                begin(
                    remote(
                        log_send.at[k],
                        log_got.at[k],
                        end_send.at[1, k],
                        end_recv.at[1, k],
                        to_blk(k),
                    )
                ),
            )
        )
    memory_ref[block] = units[block]
    logs = [log_full[0]]
    outputs = [out_send[0].astype(floats)]
    for k, copies in zip(ORDER[1:], ended):
        for copy in copies:
            copy.wait_recv()
        logs.append(wide_log(log_got[k]))
        outputs.append(out_got[k].astype(floats))
    peak = jnp.maximum(jnp.maximum(logs[0], logs[1]), jnp.maximum(logs[2], logs[3]))
    parts = [jnp.exp(one - peak) for one in logs]
    mixed = sum(part * output for part, output in zip(parts, outputs))
    answer_ref[...] = (mixed / sum(parts)).astype(jnp.bfloat16)
    for k, copy in zip(ORDER[1:], relayout):
        copy.wait_recv()
        memory_ref[partner(block, k)] = got_units[k]
    for copy in started:
        copy.wait_send()


def whole_step(
    merger_rows, out_weight, kv_weight, bias, queries, stored, retrieved, merge_map, owner_map
):
    rows = merger_rows.shape[0]
    depth, inner = out_weight.shape
    cols = kv_weight.shape[1]
    half, half_cols = rows // 2, cols // 2
    group, head_size = queries.shape[1:]
    new_count = half // UNIT_TOK
    slot_rows = 2 * ((new_count + 3) // 4) * UNIT_TOK
    kept, wide = jnp.bfloat16, jnp.float32
    macs = 4 * rows * inner * (depth + cols)
    hbm = pl.BlockSpec(memory_space=pl.ANY)
    vmem = pl.BlockSpec(memory_space=pltpu.VMEM)
    scratch = [
        ((depth, inner), kept),
        ((inner, cols), kept),
        ((4, rows, depth), kept),
        ((rows, inner), kept),
        ((4, rows, cols), kept),
        ((4, half, cols), kept),
        ((4, half, cols), kept),
        ((4, half, half_cols), kept),
        ((4, half, half_cols), kept),
        ((4, half, half_cols), kept),
        ((4, 2, group, head_size), kept),
        (stored.shape, kept),
        ((2, 4, group, head_size), wide),
        ((4, group, head_size), kept),
        ((4, group, head_size), kept),
        ((2, 4, group, head_size), wide),
        ((4, 8, head_size), wide),
        ((4, 8, head_size), wide),
        ((2, half, half_cols), kept),
        ((2, 8, 128), wide),
        ((4, slot_rows, half_cols), kept),
        ((4, slot_rows, half_cols), kept),
        ((4, group, head_size), kept),
        ((4, group, head_size), kept),
        ((4, group, head_size), wide),
        ((4, 8, head_size), wide),
        ((4, 8, head_size), wide),
    ]
    semaphores = [(4,), (4, 4), (4, 4), (3, 4), (3, 4), (2, 4), (2, 4), (4,), (4,), (3, 4), (3, 4)]
    return pl.pallas_call(
        project_kernel,
        out_shape=(
            jax.ShapeDtypeStruct((group, head_size), kept),
            jax.ShapeDtypeStruct((4, slot_rows, half_cols), kept),
        ),
        in_specs=[hbm, hbm, hbm, vmem, vmem, hbm, vmem, vmem, vmem],
        out_specs=(vmem, vmem),
        scratch_shapes=[pltpu.VMEM(shape, kind) for shape, kind in scratch]
        + [pltpu.SemaphoreType.DMA(shape) for shape in semaphores],
        compiler_params=pltpu.CompilerParams(
            collective_id=0, has_side_effects=True, vmem_limit_bytes=VMEM_BYTES
        ),
        cost_estimate=pl.CostEstimate(
            flops=2 * macs,
            bytes_accessed=2 * (rows * 4 * depth + depth * inner + inner * cols),
            transcendentals=0,
        ),
    )(merger_rows, out_weight, kv_weight, bias, queries, stored, retrieved, merge_map, owner_map)


def tiles_fit(
    merger_rows, out_weight, kv_weight, blocks, head_groups, copies, answer_rows, head_size
):
    return (
        blocks == 4
        and head_groups == 2
        and copies == 2
        and merger_rows.shape[0] % 64 == 0
        and out_weight.shape[0] % 128 == 0
        and out_weight.shape[1] % TILE == 0
        and kv_weight.shape[1] % TILE == 0
        and answer_rows == head_size == 128
        and merger_rows.shape[0] // copies <= 128
    )


def body(
    merger_rows,
    out_weight,
    kv_weight,
    kv_bias,
    merge_map,
    owner_map,
    old_memory,
    queries,
    retrieved,
):
    blocks = lax.axis_size("blk")
    copies = lax.axis_size("rep")
    head_groups = lax.axis_size("head")
    local_heads = KVH // head_groups
    width = kv_weight.shape[1] // KVH
    head_size = width // 2
    group_index = lax.axis_index("blk") * copies + lax.axis_index("rep")

    bias = kv_bias.reshape(1, -1)
    query_rows = queries.shape[1]
    per_head = queries.shape[3] // head_size
    slice_rows = query_rows // copies
    answer_rows = slice_rows * local_heads * per_head
    if tiles_fit(
        merger_rows, out_weight, kv_weight, blocks, head_groups, copies, answer_rows, head_size
    ):
        asking = queries.reshape(copies, slice_rows, local_heads, per_head, head_size)
        asking = asking.transpose(0, 2, 1, 3, 4).reshape(copies, answer_rows, head_size)
        stored = old_memory.reshape(-1, local_heads, width).transpose(1, 0, 2)
        answer, new_memory = whole_step(
            merger_rows,
            out_weight,
            kv_weight,
            bias,
            asking,
            stored,
            retrieved,
            merge_map.reshape(-1, 1),
            owner_map,
        )
        answer = answer.reshape(local_heads, slice_rows, per_head * head_size)
        return (
            answer.transpose(1, 0, 2)[None],
            new_memory.reshape(-1, UNIT_TOK, local_heads, width),
        )
    keyval = project(merger_rows, out_weight, kv_weight, blocks, head_groups, copies)
    keyval = (keyval.astype(jnp.float32) + bias).astype(jnp.bfloat16)
    asked = lax.all_gather(queries, "blk", axis=0, tiled=True)
    half_rows = keyval.shape[0]

    unit_count = half_rows // UNIT_TOK
    capacity = 2 * ((unit_count + blocks - 1) // blocks)
    owners = owner_map[:, 0]
    positions = jnp.arange(unit_count, dtype=jnp.int32)
    same_owner = owners[:, None] == owners[None, :]
    earlier = positions[None, :] < positions[:, None]
    ranks = jnp.sum((same_owner & earlier).astype(jnp.int32), axis=1)
    slots = owners * capacity + ranks
    row_slots = jnp.repeat(slots * UNIT_TOK, UNIT_TOK) + jnp.tile(
        jnp.arange(UNIT_TOK, dtype=jnp.int32), unit_count
    )
    placed_at = merge_map[0][:, None] == jnp.arange(half_rows, dtype=jnp.int32)[None, :]
    row_target = jnp.sum(jnp.where(placed_at, row_slots[:, None], 0), axis=0)
    slot_rows = blocks * capacity * UNIT_TOK
    select = row_target[None, :] == jnp.arange(slot_rows, dtype=jnp.int32)[:, None]
    send = jnp.dot(select.astype(jnp.bfloat16), keyval, preferred_element_type=jnp.float32)
    send = send.astype(jnp.bfloat16).reshape(blocks, capacity * UNIT_TOK, keyval.shape[1])
    arrived = lax.all_to_all(send, "blk", split_axis=0, concat_axis=0, tiled=True)
    new_memory = arrived.reshape(blocks * capacity, UNIT_TOK, local_heads, width)

    old_count = old_memory.shape[0]
    old_ids = group_index * old_count + jnp.arange(old_count, dtype=jnp.int32)
    new_ids = old_count * blocks * copies + group_index * unit_count + positions
    old_listed = jnp.any(retrieved[:, :, None] == old_ids[None, None, :], axis=1)
    new_listed = jnp.any(retrieved[:, :, None] == new_ids[None, None, :], axis=1)
    slot_listed = jnp.repeat(new_listed, UNIT_TOK, axis=1)
    row_listed = jnp.any(slot_listed[:, :, None] & placed_at[None], axis=1)
    mask = jnp.concatenate([jnp.repeat(old_listed, UNIT_TOK, axis=1), row_listed], axis=1)

    questions = asked.shape[0]
    asked = asked.reshape(questions, query_rows, local_heads, per_head, head_size)
    old_flat = old_memory.reshape(-1, local_heads, width)
    flat = jnp.concatenate([old_flat, keyval.reshape(half_rows, local_heads, width)], axis=0)
    keys = flat[..., :head_size]
    values = flat[..., head_size:]
    wide_mask = mask[None, :, None, None, :]
    scores = jnp.einsum("aqkhd,tkd->kaqht", asked, keys, preferred_element_type=jnp.float32)
    scores = jnp.where(wide_mask, scores * head_size ** (-0.5), -1e30)
    peak = jnp.max(scores, axis=-1)
    weights = jnp.where(wide_mask, jnp.exp(scores - peak[..., None]), 0.0)
    total = jnp.sum(weights, axis=-1)
    output = jnp.einsum(
        "kaqht,tkd->kaqhd", weights.astype(jnp.bfloat16), values, preferred_element_type=jnp.float32
    )

    def by_holder(part):
        part = part.reshape((local_heads, questions, copies, slice_rows) + part.shape[3:])
        part = jnp.moveaxis(part, 0, 3)
        return part.reshape((questions * copies, slice_rows * local_heads * per_head) + part.shape[5:])

    stat_rows = -(-answer_rows // head_size)
    spare = ((0, 0), (0, stat_rows * head_size - answer_rows))
    stats = jnp.stack([jnp.pad(by_holder(peak), spare), jnp.pad(by_holder(total), spare)], axis=1)
    partial = jnp.concatenate(
        [by_holder(output), stats.reshape(questions * copies, 2 * stat_rows, head_size)], axis=1
    )
    partial = lax.all_to_all(partial, ("blk", "rep"), split_axis=0, concat_axis=0, tiled=True)
    outputs = partial[:, :answer_rows]
    stats = partial[:, answer_rows:].reshape(-1, 2, stat_rows * head_size)[..., :answer_rows]
    scale = jnp.exp(stats[:, 0] - jnp.max(stats[:, 0], axis=0, keepdims=True))
    total = jnp.sum(stats[:, 1] * scale, axis=0)
    result = jnp.sum(outputs * scale[..., None], axis=0) / total[:, None]
    answer = result.reshape(1, slice_rows, local_heads, per_head * head_size).astype(jnp.bfloat16)
    return (answer, new_memory)


def solution(mesh):
    placed = (
        P(("groups", "blk"), None),
        P("blk", ("head", "rep")),
        P(("head", "rep"), None),
        P("head", None),
        P(("groups", "blk", "rep"), None),
        P(("groups", "blk", "rep"), None),
        P(("groups", "blk", "rep"), None, "head", None),
        P(("groups", "blk"), None, "head", None),
        P("groups", None),
    )
    return jax.shard_map(
        body,
        mesh=mesh,
        in_specs=placed,
        out_specs=(
            P(("groups", "blk"), "rep", "head", None),
            P(("groups", "blk", "rep"), None, "head", None),
        ),
        check_vma=False,
    )
```

```python
import jax
import jax.numpy as jnp
from jax import lax
from jax.experimental import pallas as pl
from jax.experimental.pallas import tpu as pltpu
from jax.sharding import PartitionSpec as P

KVH = 8
UNIT_TOK = 8


def project(merger_rows, out_weight, kv_weight, blocks, head_groups, copies):
    rows = merger_rows.shape[0]
    depth = out_weight.shape[0]
    split = merger_rows.reshape(rows, blocks, depth).transpose(1, 0, 2)
    features = lax.all_to_all(split, "blk", split_axis=0, concat_axis=0, tiled=True)
    visual = jnp.dot(
        features.reshape(blocks * rows, depth), out_weight, preferred_element_type=jnp.float32
    ).astype(jnp.bfloat16)
    partial = jnp.dot(visual, kv_weight, preferred_element_type=jnp.float32).astype(jnp.bfloat16)
    cols = kv_weight.shape[1] // head_groups
    partial = partial.reshape(blocks, copies, rows // copies, head_groups, cols)
    partial = partial.transpose(0, 3, 1, 2, 4).reshape(-1, rows // copies, cols)
    return lax.psum_scatter(
        partial, ("blk", "head", "rep"), scatter_dimension=0, tiled=True
    ).reshape(rows // copies, cols)


TILE = 512
ORDER = (0, 3, 2, 1)
VMEM_BYTES = 48 * 1024 * 1024


def partner(block, k):
    if k == 0:
        return block
    if k == 1:
        return block + 1 - 2 * (block % 2)
    if k == 2:
        return block + 2 - 4 * (block // 2)
    return 3 - block


def project_kernel(
    rows_ref,
    weight_ref,
    kv_ref,
    bias_ref,
    queries_ref,
    stored_ref,
    retrieved_ref,
    merge_ref,
    owner_ref,
    answer_ref,
    memory_ref,
    weight,
    kv,
    feats,
    visual,
    sums,
    got_rep,
    half_sums,
    got_head,
    own_sums,
    got_blk,
    asked,
    stored,
    old_out,
    old_out_send,
    old_out_got,
    old_log,
    old_log_send,
    old_log_got,
    new_rows,
    new_mask,
    units,
    got_units,
    out_send,
    out_got,
    log_full,
    log_send,
    log_got,
    local_sem,
    feat_send,
    feat_recv,
    sum_send,
    sum_recv,
    query_send,
    query_recv,
    rep_send,
    rep_recv,
    end_send,
    end_recv,
):
    block = lax.axis_index("blk")
    head = lax.axis_index("head")
    rep = lax.axis_index("rep")
    rows, depth = feats.shape[1:]
    half = rows // 2
    quarter = rows // 4
    cols = kv.shape[1]
    half_cols = cols // 2
    to_head = {"head": 1 - head}
    to_rep = {"rep": 1 - rep}

    def to_blk(k):
        return {"blk": partner(block, k)}

    def remote(src, dst, send, recv, device):
        return pltpu.make_async_remote_copy(
            src_ref=src,
            dst_ref=dst,
            send_sem=send,
            recv_sem=recv,
            device_id=device,
            device_id_type=pl.DeviceIdType.MESH,
        )

    def quarter_rows(h, r):
        return pl.ds(pl.multiple_of((h * 2 + r) * quarter, quarter), quarter)

    own_rows = quarter_rows(head, rep)
    over_head_rows = quarter_rows(1 - head, rep)

    def feature_columns(k):
        return pl.ds(pl.multiple_of(partner(block, k) * depth, depth), depth)

    load_rows = pltpu.make_async_copy(
        rows_ref.at[:, feature_columns(0)], feats.at[0], local_sem.at[0]
    )
    load_weight = pltpu.make_async_copy(weight_ref, weight, local_sem.at[1])
    load_kv = pltpu.make_async_copy(kv_ref, kv, local_sem.at[2])
    load_rows.start()
    load_weight.start()
    load_kv.start()
    load_stored = pltpu.make_async_copy(stored_ref, stored, local_sem.at[3])
    load_stored.start()

    barrier = pltpu.get_barrier_semaphore()
    for device in (to_blk(1), to_blk(2), to_blk(3), to_head, to_rep):
        pl.semaphore_signal(
            barrier, inc=1, device_id=device, device_id_type=pl.DeviceIdType.MESH
        )
    pl.semaphore_wait(barrier, 5)

    started = []

    def begin(copy):
        copy.start()
        started.append(copy)
        return copy

    over_blk, asking, ask_again = {}, {}, {}

    def send_features(k):
        over_blk[k] = begin(
            remote(
                rows_ref.at[own_rows, feature_columns(k)],
                feats.at[k, own_rows],
                feat_send.at[0, k],
                feat_recv.at[0, k],
                to_blk(k),
            )
        )

    def send_queries():
        for k in (1, 2, 3):
            asking[k] = begin(
                remote(
                    queries_ref.at[rep],
                    asked.at[k, rep],
                    query_send.at[0, k],
                    query_recv.at[0, k],
                    to_blk(k),
                )
            )

    def pass_queries():
        for k in (1, 2, 3):
            asking[k].wait_recv()
            piece = asked.at[k, rep]
            ask_again[k] = begin(
                remote(piece, piece, query_send.at[1, k], query_recv.at[1, k], to_rep)
            )

    send_features(ORDER[1])
    send_features(ORDER[2])
    send_features(ORDER[3])

    over_head, over_rep, last_rep = {}, {}, {}

    def pass_quarter(k):
        over_blk[k].wait_recv()
        piece = feats.at[k, own_rows]
        over_head[k] = begin(
            remote(piece, piece, feat_send.at[1, k], feat_recv.at[1, k], to_head)
        )
        over_rep[k] = begin(
            remote(piece, piece, feat_send.at[2, k], feat_recv.at[2, k], to_rep)
        )

    def pass_second(k):
        over_head[k].wait_recv()
        piece = feats.at[k, over_head_rows]
        last_rep[k] = begin(
            remote(piece, piece, feat_send.at[3, k], feat_recv.at[3, k], to_rep)
        )

    def have_rows(k):
        over_rep[k].wait_recv()
        last_rep[k].wait_recv()

    def multiply(k):
        @pl.loop(0, weight.shape[1] // TILE)
        def _(i):
            at = pl.ds(pl.multiple_of(i * TILE, TILE), TILE)
            visual[:, at] = jnp.dot(
                feats[k], weight[:, at], preferred_element_type=jnp.float32
            ).astype(jnp.bfloat16)

        if k == 0:
            send_queries()
            load_kv.wait()

        @pl.loop(0, cols // TILE)
        def _(i):
            at = pl.ds(pl.multiple_of(i * TILE, TILE), TILE)
            sums[k, :, at] = jnp.dot(
                visual[...], kv[:, at], preferred_element_type=jnp.float32
            ).astype(jnp.bfloat16)

    own_half = pl.ds(pl.multiple_of(rep * half, half), half)
    other_half = pl.ds(pl.multiple_of((1 - rep) * half, half), half)
    own_cols = pl.ds(pl.multiple_of(head * half_cols, half_cols), half_cols)
    other_cols = pl.ds(pl.multiple_of((1 - head) * half_cols, half_cols), half_cols)
    by_rep, by_head, by_blk = {}, {}, {}

    def send_rep(k):
        by_rep[k] = begin(
            remote(
                sums.at[k, other_half],
                got_rep.at[k],
                sum_send.at[0, k],
                sum_recv.at[0, k],
                to_rep,
            )
        )

    def send_head(k):
        by_rep[k].wait_recv()
        half_sums[k] = (
            sums[k, own_half, :].astype(jnp.float32) + got_rep[k].astype(jnp.float32)
        ).astype(jnp.bfloat16)
        by_head[k] = begin(
            remote(
                half_sums.at[k, :, other_cols],
                got_head.at[k],
                sum_send.at[1, k],
                sum_recv.at[1, k],
                to_head,
            )
        )

    def send_blk(k):
        by_head[k].wait_recv()
        own_sums[k] = (
            half_sums[k, :, own_cols].astype(jnp.float32) + got_head[k].astype(jnp.float32)
        ).astype(jnp.bfloat16)
        if k == 0:
            return
        if k == 2:
            by_blk[3].wait_recv()
            own_sums[2] = (
                own_sums[2].astype(jnp.float32) + got_blk[3].astype(jnp.float32)
            ).astype(jnp.bfloat16)
        by_blk[k] = begin(
            remote(
                own_sums.at[k],
                got_blk.at[k],
                sum_send.at[2, k],
                sum_recv.at[2, k],
                to_blk(2 if k == 2 else 1),
            )
        )

    heads = stored.shape[0]
    stored_rows = stored.shape[1]
    head_size = asked.shape[3]
    ask_rows = asked.shape[2] // heads
    group = asked.shape[2]
    new_count = half // UNIT_TOK
    scale = head_size ** (-0.5)
    place = block * 2 + rep
    floats = jnp.float32

    def iota(shape, dim):
        return lax.broadcasted_iota(jnp.int32, shape, dim)

    def listed(ids):
        units_of = jnp.concatenate(
            [retrieved_ref[pl.ds(partner(block, k), 1), :] for k in range(4)], axis=0
        )
        hit = jnp.zeros((4, ids.shape[1]), floats)
        for j in range(units_of.shape[1]):
            hit = jnp.where(ids == units_of[:, j : j + 1], 1.0, hit)
        return hit

    def row_mask(mask, count):
        return jnp.concatenate(
            [
                jnp.broadcast_to(mask[k : k + 1], (count, mask.shape[1]))
                for k in range(4)
            ],
            axis=0,
        )

    def flat_log(wide):
        return jnp.transpose(wide)[:8]

    def wide_log(flat):
        return jnp.transpose(jnp.broadcast_to(flat[:1], (group, group)))

    def prepare():
        eye = iota((new_count, new_count), 0) == iota((new_count, new_count), 1)
        owner = owner_ref[...].astype(floats)
        owner_row = jnp.sum(jnp.where(eye, owner, 0.0), axis=0, keepdims=True)
        earlier = iota((new_count, new_count), 1) < iota((new_count, new_count), 0)
        rank = jnp.sum(
            jnp.where((owner == owner_row) & earlier, 1.0, 0.0), axis=1, keepdims=True
        )
        capacity = units.shape[1] // UNIT_TOK
        slot = owner * capacity + rank
        slot_row = jnp.sum(jnp.where(eye, slot, 0.0), axis=0, keepdims=True)
        of_unit = iota((half, new_count), 0) // UNIT_TOK == iota((half, new_count), 1)
        slot_of = jnp.sum(jnp.where(of_unit, slot_row, 0.0), axis=1, keepdims=True)
        position = iota((half, 1), 0)
        target = slot_of * UNIT_TOK + (position % UNIT_TOK).astype(floats)
        fills = merge_ref[...] == iota((half, half), 1)
        target_row = jnp.sum(jnp.where(fills, target, 0.0), axis=0, keepdims=True)
        unit_of = (position // UNIT_TOK).astype(floats)
        unit_row = jnp.sum(jnp.where(fills, unit_of, 0.0), axis=0, keepdims=True)
        slots = units.shape[0] * units.shape[1]
        select = jnp.where(
            iota((slots, half), 0) == target_row.astype(jnp.int32), 1.0, 0.0
        ).astype(jnp.bfloat16)
        base = stored_rows // UNIT_TOK * 8 + place * new_count
        new_mask[0] = jnp.zeros(new_mask.shape[1:], floats)
        new_mask[0, 0:4, 0:half] = listed(base + unit_row.astype(jnp.int32))
        return select

    def attend_stored(start_head, stop_head):
        ids = place * (stored_rows // UNIT_TOK) + iota((1, stored_rows), 1) // UNIT_TOK
        mask = row_mask(listed(ids), 2 * ask_rows) > 0.0

        @pl.loop(start_head, stop_head)
        def _(h):
            at = pl.ds(pl.multiple_of(h * ask_rows, ask_rows), ask_rows)
            query = jnp.concatenate(
                [asked[k, r, at, :] for k in range(4) for r in range(2)], axis=0
            )
            scores = lax.dot_general(
                query,
                stored[h, :, :head_size],
                (((1,), (1,)), ((), ())),
                preferred_element_type=floats,
            )
            scores = jnp.where(mask, scores * scale, -1e30)
            peak = jnp.max(scores, axis=1, keepdims=True)
            weights = jnp.where(mask, jnp.exp(scores - peak), 0.0)
            total = jnp.maximum(jnp.sum(weights, axis=1, keepdims=True), 1e-30)
            output = jnp.dot(
                weights.astype(jnp.bfloat16),
                stored[h, :, head_size:],
                preferred_element_type=floats,
            )
            output = output / total
            logs = jnp.broadcast_to(peak + jnp.log(total), output.shape)
            for k in range(4):
                for r in range(2):
                    start = (2 * k + r) * ask_rows
                    old_out[r, k, at, :] = output[start : start + ask_rows]
                    old_log[r, k, at, :] = logs[start : start + ask_rows]

    old_parts = []

    def send_stored():
        old_out_send[...] = old_out[1 - rep].astype(jnp.bfloat16)
        for k in range(4):
            old_log_send[k] = flat_log(old_log[1 - rep, k])
        for i, (src, dst) in enumerate(
            (
                (old_out_send, old_out_got),
                (old_log_send, old_log_got),
                (new_mask.at[0], new_mask.at[1]),
            )
        ):
            old_parts.append(
                begin(remote(src, dst, rep_send.at[i], rep_recv.at[i], to_rep))
            )

    def merge_stored():
        for copy in old_parts:
            copy.wait_recv()
        for k in range(4):
            mine, theirs = old_log[rep, k], wide_log(old_log_got[k])
            peak = jnp.maximum(mine, theirs)
            first_part, second_part = jnp.exp(mine - peak), jnp.exp(theirs - peak)
            total = first_part + second_part
            old_out[rep, k] = (
                first_part * old_out[rep, k] + second_part * old_out_got[k].astype(floats)
            ) / total
            old_log[rep, k] = peak + jnp.log(total)

    def attend_new():
        masks = [row_mask(new_mask[i, 0:4, 0:half], ask_rows) > 0.0 for i in range(2)]

        @pl.loop(0, heads)
        def _(h):
            at = pl.ds(pl.multiple_of(h * ask_rows, ask_rows), ask_rows)
            key_at = pl.ds(pl.multiple_of(h * 2 * head_size, head_size), head_size)
            value_at = pl.ds(
                pl.multiple_of(h * 2 * head_size + head_size, head_size), head_size
            )
            query = jnp.concatenate([asked[k, rep, at, :] for k in range(4)], axis=0)
            before = jnp.concatenate([old_log[rep, k, at, :] for k in range(4)], axis=0)
            output = jnp.concatenate([old_out[rep, k, at, :] for k in range(4)], axis=0)
            peak, scores = before, []
            for i in range(2):
                part = lax.dot_general(
                    query,
                    new_rows[i, :, key_at],
                    (((1,), (1,)), ((), ())),
                    preferred_element_type=floats,
                )
                part = jnp.where(masks[i], part * scale, -1e30)
                scores.append(part)
                peak = jnp.maximum(peak, jnp.max(part, axis=1, keepdims=True))
            total = jnp.exp(before - peak)
            output = output * total
            for i in range(2):
                weights = jnp.where(masks[i], jnp.exp(scores[i] - peak[:, :half]), 0.0)
                total = total + jnp.sum(weights, axis=1, keepdims=True)
                output = output + jnp.dot(
                    weights.astype(jnp.bfloat16),
                    new_rows[i, :, value_at],
                    preferred_element_type=floats,
                )
            total = jnp.maximum(total, 1e-30)
            output = output / total
            logs = peak + jnp.log(total)
            for k in range(4):
                part = slice(k * ask_rows, (k + 1) * ask_rows)
                out_send[k, at, :] = output[part].astype(jnp.bfloat16)
                log_full[k, at, :] = logs[part]

    first, second, third, fourth = ORDER
    load_rows.wait()
    load_weight.wait()
    multiply(first)
    send_rep(first)
    pass_quarter(second)
    pass_second(second)
    select = prepare()
    asked[0] = queries_ref[...]
    send_head(first)
    pass_queries()
    pass_quarter(third)
    have_rows(second)
    multiply(second)
    send_rep(second)
    pass_second(third)
    send_head(second)
    send_blk(first)
    pass_quarter(fourth)
    have_rows(third)
    multiply(third)
    send_rep(third)
    pass_second(fourth)
    send_head(third)
    send_blk(second)
    have_rows(fourth)
    multiply(fourth)
    send_rep(fourth)
    send_blk(third)
    send_head(fourth)
    load_stored.wait()
    for copy in ask_again.values():
        copy.wait_recv()
    attend_stored(0, heads // 2)
    send_blk(fourth)
    attend_stored(heads // 2, heads)
    send_stored()

    total = own_sums[0].astype(floats) + bias_ref[...]
    for k in (2, 1):
        by_blk[k].wait_recv()
        total = total + got_blk[k].astype(floats)
    new_rows[0] = total.astype(jnp.bfloat16)
    share = begin(
        remote(new_rows.at[0], new_rows.at[1], rep_send.at[3], rep_recv.at[3], to_rep)
    )
    units[...] = (
        jnp.dot(select, new_rows[0], preferred_element_type=floats)
        .astype(jnp.bfloat16)
        .reshape(units.shape)
    )
    relayout = []
    for k in ORDER[1:]:
        relayout.append(
            begin(
                remote(
                    units.at[partner(block, k)],
                    got_units.at[k],
                    end_send.at[2, k],
                    end_recv.at[2, k],
                    to_blk(k),
                )
            )
        )
    merge_stored()
    share.wait_recv()
    attend_new()
    ended = []
    for k in ORDER[1:]:
        log_send[k] = flat_log(log_full[k])
        ended.append(
            (
                begin(
                    remote(
                        out_send.at[k],
                        out_got.at[k],
                        end_send.at[0, k],
                        end_recv.at[0, k],
                        to_blk(k),
                    )
                ),
                begin(
                    remote(
                        log_send.at[k],
                        log_got.at[k],
                        end_send.at[1, k],
                        end_recv.at[1, k],
                        to_blk(k),
                    )
                ),
            )
        )
    memory_ref[block] = units[block]
    logs = [log_full[0]]
    outputs = [out_send[0].astype(floats)]
    for k, copies in zip(ORDER[1:], ended):
        for copy in copies:
            copy.wait_recv()
        logs.append(wide_log(log_got[k]))
        outputs.append(out_got[k].astype(floats))
    peak = jnp.maximum(jnp.maximum(logs[0], logs[1]), jnp.maximum(logs[2], logs[3]))
    parts = [jnp.exp(one - peak) for one in logs]
    mixed = sum(part * output for part, output in zip(parts, outputs))
    answer_ref[...] = (mixed / sum(parts)).astype(jnp.bfloat16)
    for k, copy in zip(ORDER[1:], relayout):
        copy.wait_recv()
        memory_ref[partner(block, k)] = got_units[k]
    for copy in started:
        copy.wait_send()


def whole_step(
    merger_rows, out_weight, kv_weight, bias, queries, stored, retrieved, merge_map, owner_map
):
    rows = merger_rows.shape[0]
    depth, inner = out_weight.shape
    cols = kv_weight.shape[1]
    half, half_cols = rows // 2, cols // 2
    group, head_size = queries.shape[1:]
    new_count = half // UNIT_TOK
    slot_rows = 2 * ((new_count + 3) // 4) * UNIT_TOK
    kept, wide = jnp.bfloat16, jnp.float32
    macs = 4 * rows * inner * (depth + cols)
    hbm = pl.BlockSpec(memory_space=pl.ANY)
    vmem = pl.BlockSpec(memory_space=pltpu.VMEM)
    scratch = [
        ((depth, inner), kept),
        ((inner, cols), kept),
        ((4, rows, depth), kept),
        ((rows, inner), kept),
        ((4, rows, cols), kept),
        ((4, half, cols), kept),
        ((4, half, cols), kept),
        ((4, half, half_cols), kept),
        ((4, half, half_cols), kept),
        ((4, half, half_cols), kept),
        ((4, 2, group, head_size), kept),
        (stored.shape, kept),
        ((2, 4, group, head_size), wide),
        ((4, group, head_size), kept),
        ((4, group, head_size), kept),
        ((2, 4, group, head_size), wide),
        ((4, 8, head_size), wide),
        ((4, 8, head_size), wide),
        ((2, half, half_cols), kept),
        ((2, 8, 128), wide),
        ((4, slot_rows, half_cols), kept),
        ((4, slot_rows, half_cols), kept),
        ((4, group, head_size), kept),
        ((4, group, head_size), kept),
        ((4, group, head_size), wide),
        ((4, 8, head_size), wide),
        ((4, 8, head_size), wide),
    ]
    semaphores = [(4,), (4, 4), (4, 4), (3, 4), (3, 4), (2, 4), (2, 4), (4,), (4,), (3, 4), (3, 4)]
    return pl.pallas_call(
        project_kernel,
        out_shape=(
            jax.ShapeDtypeStruct((group, head_size), kept),
            jax.ShapeDtypeStruct((4, slot_rows, half_cols), kept),
        ),
        in_specs=[hbm, hbm, hbm, vmem, vmem, hbm, vmem, vmem, vmem],
        out_specs=(vmem, vmem),
        scratch_shapes=[pltpu.VMEM(shape, kind) for shape, kind in scratch]
        + [pltpu.SemaphoreType.DMA(shape) for shape in semaphores],
        compiler_params=pltpu.CompilerParams(
            collective_id=0, has_side_effects=True, vmem_limit_bytes=VMEM_BYTES
        ),
        cost_estimate=pl.CostEstimate(
            flops=2 * macs,
            bytes_accessed=2 * (rows * 4 * depth + depth * inner + inner * cols),
            transcendentals=0,
        ),
    )(merger_rows, out_weight, kv_weight, bias, queries, stored, retrieved, merge_map, owner_map)


def tiles_fit(
    merger_rows, out_weight, kv_weight, blocks, head_groups, copies, answer_rows, head_size
):
    return (
        blocks == 4
        and head_groups == 2
        and copies == 2
        and merger_rows.shape[0] % 64 == 0
        and out_weight.shape[0] % 128 == 0
        and out_weight.shape[1] % TILE == 0
        and kv_weight.shape[1] % TILE == 0
        and answer_rows == head_size == 128
        and merger_rows.shape[0] // copies <= 128
    )


def body(
    merger_rows,
    out_weight,
    kv_weight,
    kv_bias,
    merge_map,
    owner_map,
    old_memory,
    queries,
    retrieved,
):
    blocks = lax.axis_size("blk")
    copies = lax.axis_size("rep")
    head_groups = lax.axis_size("head")
    local_heads = KVH // head_groups
    width = kv_weight.shape[1] // KVH
    head_size = width // 2
    group_index = lax.axis_index("blk") * copies + lax.axis_index("rep")

    bias = kv_bias.reshape(1, -1)
    query_rows = queries.shape[1]
    per_head = queries.shape[3] // head_size
    slice_rows = query_rows // copies
    answer_rows = slice_rows * local_heads * per_head
    if tiles_fit(
        merger_rows, out_weight, kv_weight, blocks, head_groups, copies, answer_rows, head_size
    ):
        asking = queries.reshape(copies, slice_rows, local_heads, per_head, head_size)
        asking = asking.transpose(0, 2, 1, 3, 4).reshape(copies, answer_rows, head_size)
        stored = old_memory.reshape(-1, local_heads, width).transpose(1, 0, 2)
        answer, new_memory = whole_step(
            merger_rows,
            out_weight,
            kv_weight,
            bias,
            asking,
            stored,
            retrieved,
            merge_map.reshape(-1, 1),
            owner_map,
        )
        answer = answer.reshape(local_heads, slice_rows, per_head * head_size)
        return (
            answer.transpose(1, 0, 2)[None],
            new_memory.reshape(-1, UNIT_TOK, local_heads, width),
        )
    keyval = project(merger_rows, out_weight, kv_weight, blocks, head_groups, copies)
    keyval = (keyval.astype(jnp.float32) + bias).astype(jnp.bfloat16)
    asked = lax.all_gather(queries, "blk", axis=0, tiled=True)
    half_rows = keyval.shape[0]

    unit_count = half_rows // UNIT_TOK
    capacity = 2 * ((unit_count + blocks - 1) // blocks)
    owners = owner_map[:, 0]
    positions = jnp.arange(unit_count, dtype=jnp.int32)
    same_owner = owners[:, None] == owners[None, :]
    earlier = positions[None, :] < positions[:, None]
    ranks = jnp.sum((same_owner & earlier).astype(jnp.int32), axis=1)
    slots = owners * capacity + ranks
    row_slots = jnp.repeat(slots * UNIT_TOK, UNIT_TOK) + jnp.tile(
        jnp.arange(UNIT_TOK, dtype=jnp.int32), unit_count
    )
    placed_at = merge_map[0][:, None] == jnp.arange(half_rows, dtype=jnp.int32)[None, :]
    row_target = jnp.sum(jnp.where(placed_at, row_slots[:, None], 0), axis=0)
    slot_rows = blocks * capacity * UNIT_TOK
    select = row_target[None, :] == jnp.arange(slot_rows, dtype=jnp.int32)[:, None]
    send = jnp.dot(select.astype(jnp.bfloat16), keyval, preferred_element_type=jnp.float32)
    send = send.astype(jnp.bfloat16).reshape(blocks, capacity * UNIT_TOK, keyval.shape[1])
    arrived = lax.all_to_all(send, "blk", split_axis=0, concat_axis=0, tiled=True)
    new_memory = arrived.reshape(blocks * capacity, UNIT_TOK, local_heads, width)

    old_count = old_memory.shape[0]
    old_ids = group_index * old_count + jnp.arange(old_count, dtype=jnp.int32)
    new_ids = old_count * blocks * copies + group_index * unit_count + positions
    old_listed = jnp.any(retrieved[:, :, None] == old_ids[None, None, :], axis=1)
    new_listed = jnp.any(retrieved[:, :, None] == new_ids[None, None, :], axis=1)
    slot_listed = jnp.repeat(new_listed, UNIT_TOK, axis=1)
    row_listed = jnp.any(slot_listed[:, :, None] & placed_at[None], axis=1)
    mask = jnp.concatenate([jnp.repeat(old_listed, UNIT_TOK, axis=1), row_listed], axis=1)

    questions = asked.shape[0]
    asked = asked.reshape(questions, query_rows, local_heads, per_head, head_size)
    old_flat = old_memory.reshape(-1, local_heads, width)
    flat = jnp.concatenate([old_flat, keyval.reshape(half_rows, local_heads, width)], axis=0)
    keys = flat[..., :head_size]
    values = flat[..., head_size:]
    wide_mask = mask[None, :, None, None, :]
    scores = jnp.einsum("aqkhd,tkd->kaqht", asked, keys, preferred_element_type=jnp.float32)
    scores = jnp.where(wide_mask, scores * head_size ** (-0.5), -1e30)
    peak = jnp.max(scores, axis=-1)
    weights = jnp.where(wide_mask, jnp.exp(scores - peak[..., None]), 0.0)
    total = jnp.sum(weights, axis=-1)
    output = jnp.einsum(
        "kaqht,tkd->kaqhd", weights.astype(jnp.bfloat16), values, preferred_element_type=jnp.float32
    )

    def by_holder(part):
        part = part.reshape((local_heads, questions, copies, slice_rows) + part.shape[3:])
        part = jnp.moveaxis(part, 0, 3)
        return part.reshape((questions * copies, slice_rows * local_heads * per_head) + part.shape[5:])

    stat_rows = -(-answer_rows // head_size)
    spare = ((0, 0), (0, stat_rows * head_size - answer_rows))
    stats = jnp.stack([jnp.pad(by_holder(peak), spare), jnp.pad(by_holder(total), spare)], axis=1)
    partial = jnp.concatenate(
        [by_holder(output), stats.reshape(questions * copies, 2 * stat_rows, head_size)], axis=1
    )
    partial = lax.all_to_all(partial, ("blk", "rep"), split_axis=0, concat_axis=0, tiled=True)
    outputs = partial[:, :answer_rows]
    stats = partial[:, answer_rows:].reshape(-1, 2, stat_rows * head_size)[..., :answer_rows]
    scale = jnp.exp(stats[:, 0] - jnp.max(stats[:, 0], axis=0, keepdims=True))
    total = jnp.sum(stats[:, 1] * scale, axis=0)
    result = jnp.sum(outputs * scale[..., None], axis=0) / total[:, None]
    answer = result.reshape(1, slice_rows, local_heads, per_head * head_size).astype(jnp.bfloat16)
    return (answer, new_memory)


def solution(mesh):
    placed = (
        P(("groups", "blk"), None),
        P("blk", ("head", "rep")),
        P(("head", "rep"), None),
        P("head", None),
        P(("groups", "blk", "rep"), None),
        P(("groups", "blk", "rep"), None),
        P(("groups", "blk", "rep"), None, "head", None),
        P(("groups", "blk"), None, "head", None),
        P("groups", None),
    )
    return jax.shard_map(
        body,
        mesh=mesh,
        in_specs=placed,
        out_specs=(
            P(("groups", "blk"), "rep", "head", None),
            P(("groups", "blk", "rep"), None, "head", None),
        ),
        check_vma=False,
    )
```
